512 devices in a mesh: tm: 32 (over y_lo, x, core), heads: 16 (over z, y_hi).
Axes of the slice: x: 4, y: 8 (y_hi: 2, y_lo: 4; y = y_hi * 4 + y_lo), z: 8, core: 2. Of those that a mesh axis runs over, the one named last changes fastest.
Arguments:
- layer_input: bfloat16 [4096, 8192], P('tm', 'heads'), may hold values from -0.119628906 to 0.119628906
- proj_weight: bfloat16 [2048, 8192], P('tm', 'heads'), may hold values from -0.0625 to 0.0625
- ssd_input: float32 [4096, 8192], P('tm', 'heads'), may hold values from -0.036 to 0.036
- log_decay: float32 [4096, 128], P('tm', 'heads'), may hold values from -1 to 0, as said below
- out_grad: float32 [4096, 8192], P('tm', 'heads'), may hold values from -15 to 15
Outputs:
- grad_x: float32 [4096, 8192], P('tm', 'heads')
- grad_log: float32 [4096, 128], P('tm', 'heads')
- grad_input: bfloat16 [4096, 8192], P('tm', 'heads')
- grad_weight: float32 [2048, 8192], P('tm', 'heads')
The draws below stay inside these ranges and needn't reach their ends.
Inputs may be any that keep to these rules, and one draw needn't show every extreme that they name: `log_decay`: all entries are negative.
All inputs are finite; a program needn't handle non-finite values.
Results may differ from the reference program's by a relative error of at most 0.023.
Values may be sent and summed in bfloat16 or wider, within the bound.
No kernel may reach another device: no remote copies, remote signals or barrier semaphores. Data moves between devices by JAX's collectives and lax.ppermute only.
A program may use at most 64 MiB of HBM per device.

```python
import jax
import jax.numpy as jnp
from jax import lax

D = 8192
N = 128
P_SIZE = 64
SPAN = 128
TOK_DEV = 128
TOKEN_TOTAL = 4096
HEAD_TOTAL = 128
GROUPS = 8


def draw_log_decay(key, part):
    key = jax.random.fold_in(key, 7)
    random_keys = jax.random.split(key, 7)
    fast_share = 0.5
    fast = jax.random.bernoulli(random_keys[0], fast_share, (HEAD_TOTAL,))
    fast_rate = jnp.exp(jax.random.uniform(random_keys[1], (HEAD_TOTAL,), jnp.float32, jnp.log(1.0 / 50.0), jnp.log(1.0 / 30.0)))
    slow_rate = jnp.exp(jax.random.uniform(random_keys[2], (HEAD_TOTAL,), jnp.float32, jnp.log(0.01), jnp.log(0.05))) * 2.3 / TOKEN_TOTAL
    baseline_rate = jnp.where(fast, fast_rate, slow_rate)
    history_factor = jnp.exp(jax.random.uniform(random_keys[3], (TOKEN_TOTAL // TOK_DEV, HEAD_TOTAL), jnp.float32, jnp.log(0.5), jnp.log(2.0)))
    history_factor = jnp.repeat(history_factor, TOK_DEV, axis=0)
    coarse_estimate = jax.random.uniform(random_keys[4], (TOKEN_TOTAL, HEAD_TOTAL), jnp.float32, 0.5, 1.5)
    spike_position = jax.random.randint(random_keys[5], (3, HEAD_TOTAL), 0, TOKEN_TOTAL)
    time_steps = jnp.arange(TOKEN_TOTAL)
    spike_mask = jnp.any(time_steps[:, None, None] == spike_position[None, :, :], axis=1)
    spike_logarithm = jnp.log(jax.random.uniform(random_keys[6], (TOKEN_TOTAL, HEAD_TOTAL), jnp.float32, 0.5, 0.8))
    value_rows = -baseline_rate[None, :] * history_factor * coarse_estimate + jnp.where(spike_mask, spike_logarithm, 0.0)
    return value_rows.astype(jnp.float32)


def levels(stream_key, dims, shards, low, top_value):
    def one(dim, shards_of):
        heights = jax.random.uniform(jax.random.fold_in(jax.random.fold_in(stream_key, 6), dim), (shards_of,), jnp.float32, low / len(shards), top_value / len(shards))
        return jnp.repeat(jnp.exp(heights), dims[dim] // shards_of).reshape((-1,) + (1,) * (len(dims) - dim - 1))

    gain = one(*shards[0])
    for cut in shards[1:]:
        gain = gain * one(*cut)
    return gain


def centred(rng, extent, width, most, cuts=(), dtype=jnp.bfloat16):
    drawn = jax.random.normal(rng, extent, jnp.float32) * width
    if len(cuts) > 0:
        drawn = levels(rng, extent, cuts, -0.22, 0.18) * drawn
    return jnp.clip(drawn, min=-most, max=most).astype(dtype)


def setup_inputs(seed: int = 0) -> dict:
    streams_of = jax.random.split(jax.random.key(seed), 6)
    layer_input = centred(streams_of[0], (TOKEN_TOTAL, D), 0.02, 0.119628906, ((0, 32), (1, 16)))
    proj_weight = centred(streams_of[1], (2 * GROUPS * N, D), D ** -0.5, 0.0625, ((0, 32), (1, 16)))
    ssd_input = centred(streams_of[2], (TOKEN_TOTAL, HEAD_TOTAL * P_SIZE), 0.006, 0.036, ((0, 32), (1, 16)), jnp.float32)
    log_decay = draw_log_decay(jax.random.fold_in(streams_of[5], 71), 0)
    out_grad = centred(streams_of[4], (TOKEN_TOTAL, HEAD_TOTAL * P_SIZE), 2.5, 15.0, ((0, 32), (1, 16)), jnp.float32)
    return {"layer_input": layer_input, "proj_weight": proj_weight, "ssd_input": ssd_input, "log_decay": log_decay, "out_grad": out_grad}


highest = lax.Precision.HIGHEST


def span_sums(inputs, out_grads, logs, b_rows, c_rows):
    positions = jnp.arange(inputs.shape[0])
    lower_ones = (positions[:, None] >= positions[None, :]).astype(jnp.float32)
    cumlog = jnp.dot(lower_ones, logs, precision=highest)
    decay_sum = cumlog[-1]
    head_state = jnp.einsum('jn,jh,jhp->hnp', b_rows, jnp.exp(decay_sum[None] - cumlog), inputs, precision=highest)
    grad_state = jnp.einsum('in,ih,ihp->hnp', c_rows, jnp.exp(cumlog), out_grads, precision=highest)
    return decay_sum, head_state, grad_state


def span_grads(inputs, out_grads, logs, b_rows, c_rows, state_in, grad_out):
    positions = jnp.arange(inputs.shape[0])
    causal = positions[:, None] >= positions[None, :]
    lower_ones = causal.astype(jnp.float32)
    strict_ones = (positions[:, None] < positions[None, :]).astype(jnp.float32)
    cumlog = jnp.dot(lower_ones, logs, precision=highest)
    decay_sum = cumlog[-1]
    log_gaps = cumlog.T[:, :, None] - cumlog.T[:, None, :]
    decay_mat = jnp.where(causal[None], jnp.exp(jnp.minimum(log_gaps, 0.0)), 0.0)
    inner_cb = jnp.dot(c_rows, b_rows.T, precision=highest)
    inner_gx = jnp.einsum('ihp,jhp->hij', out_grads, inputs, precision=highest)
    decayed_cb = decay_mat * inner_cb[None]
    decayed_gx = decay_mat * inner_gx
    to_end = jnp.exp(decay_sum[None] - cumlog)
    from_start = jnp.exp(cumlog)
    b_state = jnp.einsum('jn,hnp->jhp', b_rows, grad_out, precision=highest)
    c_state = jnp.einsum('in,hnp->ihp', c_rows, state_in, precision=highest)
    grad_in = jnp.einsum('hij,ihp->jhp', decayed_cb, out_grads, precision=highest) + to_end[:, :, None] * b_state
    x_state = jnp.einsum('jhp,hnp->jhn', inputs, grad_out, precision=highest)
    grad_b = jnp.einsum('hij,in->jn', decayed_gx, c_rows, precision=highest) + jnp.einsum('jh,jhn->jn', to_end, x_state, precision=highest)
    g_state = jnp.einsum('ihp,hnp->ihn', out_grads, state_in, precision=highest)
    grad_c = jnp.einsum('hij,jn->in', decayed_gx, b_rows, precision=highest) + jnp.einsum('ih,ihn->in', from_start, g_state, precision=highest)
    pair_weight = decayed_cb * inner_gx
    prefix_sum = jnp.einsum('hij,jt->hit', pair_weight, strict_ones, precision=highest)
    inside = jnp.einsum('it,hit->th', lower_ones, prefix_sum, precision=highest)
    earlier = from_start * jnp.sum(c_state * out_grads, axis=2)
    later_terms = to_end * jnp.sum(b_state * inputs, axis=2)
    across = jnp.sum(grad_out * state_in, axis=(1, 2)) * jnp.exp(decay_sum)
    grad_log = inside + jnp.dot(lower_ones.T, earlier, precision=highest) + jnp.dot(strict_ones.T, later_terms, precision=highest) + across[None]
    return grad_in, grad_log, grad_b, grad_c


def reference(layer_input, proj_weight, ssd_input, log_decay, out_grad):
    bc_full = jnp.dot(layer_input, proj_weight.T, preferred_element_type=jnp.float32)
    groups = bc_full.shape[1] // (2 * N)
    per_group = HEAD_TOTAL // groups
    spans = TOKEN_TOTAL // SPAN
    inputs = ssd_input.reshape(spans, SPAN, groups, per_group, P_SIZE)
    out_grads = out_grad.reshape(spans, SPAN, groups, per_group, P_SIZE)
    logs = log_decay.reshape(spans, SPAN, groups, per_group)
    split_bc = bc_full.reshape(spans, SPAN, groups, 2, N)
    b_rows = split_bc[:, :, :, 0]
    c_rows = split_bc[:, :, :, 1]
    sums_fn = jax.vmap(span_sums, in_axes=(1, 1, 1, 1, 1))
    grads_fn = jax.vmap(span_grads, in_axes=(1, 1, 1, 1, 1, 0, 0), out_axes=(1, 1, 1, 1))
    zero_state = jnp.zeros((groups, per_group, N, P_SIZE), jnp.float32)
    items = (inputs, out_grads, logs, b_rows, c_rows)

    def forward(carry, item):
        decay_sum, head_state, grad_state = sums_fn(*item)
        return jnp.exp(decay_sum)[:, :, None, None] * carry + head_state, carry

    def backward(carry, item):
        decay_sum, head_state, grad_state = sums_fn(*item)
        return jnp.exp(decay_sum)[:, :, None, None] * carry + grad_state, carry

    _, states = lax.scan(forward, zero_state, items)
    _, grads = lax.scan(backward, zero_state, items, reverse=True)
    results = lax.map(lambda item: grads_fn(*item), (inputs, out_grads, logs, b_rows, c_rows, states, grads))
    grad_x = results[0].reshape(TOKEN_TOTAL, HEAD_TOTAL * P_SIZE)
    grad_log = results[1].reshape(TOKEN_TOTAL, HEAD_TOTAL)
    grad_bc = jnp.stack([results[2], results[3]], axis=3).reshape(TOKEN_TOTAL, groups * 2 * N).astype(jnp.bfloat16)
    grad_input = jnp.dot(grad_bc, proj_weight, preferred_element_type=jnp.float32).astype(jnp.bfloat16)
    grad_weight = jnp.dot(grad_bc.T, layer_input, preferred_element_type=jnp.float32)
    return grad_x, grad_log, grad_input, grad_weight
```

```python
import jax
import jax.numpy as jnp
from jax import lax
from jax.experimental import pallas as pl
from jax.experimental.pallas import tpu as pltpu
from jax.sharding import Mesh
from jax.sharding import PartitionSpec as P

N = 128
EXTRA_ROWS = 8
LN2 = 0.6931471805599453
F32 = jnp.float32
BF16 = jnp.bfloat16
F16 = jnp.float16
HIGHEST = lax.Precision.HIGHEST
TM = ("ylo", "x", "core")
HEADS = ("z", "yhi")


def dot(a, b, precision=None):
    return jnp.dot(a, b, preferred_element_type=F32, precision=precision)


def dot_nt(a, b, precision=None):
    return lax.dot_general(
        a, b, (((1,), (1,)), ((), ())), preferred_element_type=F32, precision=precision
    )


def dot_tn(a, b):
    return lax.dot_general(a, b, (((0,), (0,)), ((), ())), preferred_element_type=F32)


def split(a):
    high = a.astype(BF16)
    return high, (a - high.astype(F32)).astype(BF16)


def dot_split(a, b):
    a_high, a_low = split(a)
    b_high, b_low = split(b)
    return dot(a_high, b_high) + dot(a_low, b_high) + dot(a_high, b_low)


def three_terms(row):
    high = row.astype(BF16).astype(F32)
    middle = (row - high).astype(BF16).astype(F32)
    low = row - high - middle
    term = lax.broadcasted_iota(jnp.int32, (EXTRA_ROWS, N), 0)
    return jnp.where(
        term == 0, high, jnp.where(term == 1, middle, jnp.where(term == 2, low, 0.0))
    )


def exponent_of(a):
    top = jnp.max(jnp.max(jnp.abs(a), axis=1, keepdims=True), axis=0, keepdims=True)
    return jnp.ceil(jnp.log(jnp.maximum(top, 1e-30)) * (1.0 / LN2)) - 14.0


def power(exponent):
    return jnp.exp(exponent * LN2)


def iotas(n):
    return (
        lax.broadcasted_iota(jnp.int32, (n, n), 0),
        lax.broadcasted_iota(jnp.int32, (n, n), 1),
    )


def head_spread(heads, width):
    size = width // heads
    row = lax.broadcasted_iota(jnp.int32, (heads, width), 0)
    col = lax.broadcasted_iota(jnp.int32, (heads, width), 1)
    return ((col >= row * size) & (col < (row + 1) * size)).astype(F32)


def call(kernel, outs, flops, *args, smem=0, late=()):
    several = isinstance(outs, tuple)
    out_list = outs if several else (outs,)
    read = sum(a.size * a.dtype.itemsize for a in args)
    wrote = sum(o.size * o.dtype.itemsize for o in out_list)
    spaces = [pltpu.SMEM if k < smem else pltpu.VMEM for k in range(len(args))]
    for k in late:
        spaces[k] = pl.ANY
    scratch = [pltpu.VMEM(args[k].shape, args[k].dtype) for k in late]
    if late:
        scratch.append(pltpu.SemaphoreType.DMA((len(late),)))

    def body(*refs):
        refs = list(refs)
        buffers = refs[len(args) + len(out_list) :]
        copies = [
            pltpu.make_async_copy(refs[k], buffers[i], buffers[-1].at[i])
            for i, k in enumerate(late)
        ]
        for copy in copies:
            copy.start()
        for copy in copies:
            copy.wait()
        for i, k in enumerate(late):
            refs[k] = buffers[i]
        kernel(*refs[: len(args) + len(out_list)])

    return pl.pallas_call(
        body,
        out_shape=outs,
        in_specs=[pl.BlockSpec(memory_space=space) for space in spaces],
        out_specs=jax.tree.map(lambda _: pl.BlockSpec(memory_space=pltpu.VMEM), outs),
        scratch_shapes=scratch,
        cost_estimate=pl.CostEstimate(
            flops=flops, bytes_accessed=read + wrote, transcendentals=0
        ),
        compiler_params=pltpu.CompilerParams(vmem_limit_bytes=16 * 2**20),
    )(*args)


def decay_sums(log_ref, logt_ref):
    row, col = iotas(log_ref.shape[0])
    cum = dot((row >= col).astype(F32), log_ref[...], HIGHEST)
    cumt = dot(logt_ref[...], (row <= col).astype(F32), HIGHEST)
    return cum, cumt


def decay_factors(cum, width):
    spread = head_spread(cum.shape[1], width)
    last = cum[cum.shape[0] - 1 :, :]
    return dot(jnp.exp(last - cum), spread, HIGHEST), dot(jnp.exp(cum), spread, HIGHEST)


def prepare(x_ref, dy_ref, log_ref, logt_ref, xe_ref, dyf_ref, xet_ref, dyft_ref, ds_ref):
    steps = log_ref.shape[0]
    cum, cumt = decay_sums(log_ref, logt_ref)
    to_end, from_start = decay_factors(cum, x_ref.shape[1])
    xe = x_ref[...] * to_end
    dyf = dy_ref[...] * from_start
    xe_ref[...] = xe.astype(BF16)
    dyf_ref[...] = dyf.astype(BF16)
    xet_ref[...] = xe.T
    dyft_ref[...] = dyf.T
    ds_ref[...] = jnp.broadcast_to(cumt[:, steps - 1 : steps], ds_ref.shape)


def blocks_of(first, own_ref, other_ref, group, lines):
    column, half = divmod(group, 2)
    rows = []
    for line in (2 * half, 2 * half + 1):
        at = line * lines + column
        own, other = own_ref[at], other_ref[at]
        rows += [jnp.where(first, own, other), jnp.where(first, other, own)]
    return jnp.concatenate(rows, axis=0)


def partial_kernel(core_ref, x_ref, own_ref, other_ref, out_ref):
    first = core_ref[0] == 0
    x = x_ref[...]
    steps = x.shape[0]
    groups, _, columns = out_ref.shape
    top = jnp.zeros((steps, columns), F32)
    for group in range(groups):
        part = dot_nt(x, blocks_of(first, own_ref, other_ref, group, groups // 2))
        top = jnp.maximum(top, jnp.abs(part))
        out_ref[group, :steps, :] = part
    exponent = exponent_of(top)
    scale = power(-exponent)
    for group in range(groups):
        out_ref[group, :steps, :] = out_ref[group, :steps, :] * scale
        out_ref[group, steps:, :] = jnp.broadcast_to(exponent, (EXTRA_ROWS, columns))


def sum_kernel(pieces_ref, out_ref):
    pieces, rows, columns = pieces_ref.shape
    steps = rows - EXTRA_ROWS
    exponents = [pieces_ref[k, steps:, :] for k in range(pieces)]
    top = exponents[0]
    for exponent in exponents[1:]:
        top = jnp.maximum(top, exponent)
    top = top + jnp.ceil(jnp.log(1.0 * pieces) / LN2)
    total = jnp.zeros((steps, columns), F32)
    for k in range(pieces):
        total = total + pieces_ref[k, :steps, :] * power(exponents[k] - top)[:1, :]
    out_ref[:steps, :] = total
    out_ref[steps:, :] = top


def whole_bc(own_ref, other_ref):
    steps = own_ref.shape[0] - EXTRA_ROWS
    bc = own_ref[:steps, :] * power(own_ref[steps : steps + 1, :])
    bc = bc + other_ref[:steps, :] * power(other_ref[steps : steps + 1, :])
    return bc[:, :N], bc[:, N:]


def states_kernel(own_ref, other_ref, xet_ref, dyft_ref, ds_ref, out_ref):
    b_rows, c_rows = whole_bc(own_ref, other_ref)
    heads = ds_ref.shape[0]
    parts, rows, _ = out_ref.shape
    half = (rows - EXTRA_ROWS) // 2
    state = dot_split(xet_ref[...], b_rows)
    grad = dot_split(dyft_ref[...], c_rows)
    state_exponent = exponent_of(state)
    grad_exponent = exponent_of(grad)
    out_ref[:, :half, :] = (state * power(-state_exponent)).reshape(parts, half, N)
    out_ref[:, half : 2 * half, :] = (grad * power(-grad_exponent)).reshape(parts, half, N)
    row = lax.broadcasted_iota(jnp.int32, (EXTRA_ROWS, N), 0)
    for head in range(heads):
        terms = jnp.where(row == 3, state_exponent, three_terms(ds_ref[head : head + 1, :]))
        terms = jnp.where(row == 4, grad_exponent, terms)
        for part in range(head * parts // heads, (head + 1) * parts // heads):
            out_ref[part, 2 * half :, :] = terms


def local_kernel(own_ref, other_ref, x_ref, dy_ref, log_ref, logt_ref, gx_ref, grad_ref, inside_ref):
    b_rows, c_rows = (rows.astype(BF16) for rows in whole_bc(own_ref, other_ref))
    steps, heads = log_ref.shape
    size = x_ref.shape[1] // heads
    row, col = iotas(steps)
    later = row <= col
    at_or_after = (row >= col).astype(BF16)
    bct = dot_nt(b_rows, c_rows)
    pair_sum = jnp.zeros((steps, steps), F32)
    cum, cumt = decay_sums(log_ref, logt_ref)
    for h in range(heads):
        x = x_ref[:, h * size : (h + 1) * size].astype(BF16)
        dy = dy_ref[:, h * size : (h + 1) * size].astype(BF16)
        gap = cumt[h : h + 1, :] - cum[:, h : h + 1]
        decay = jnp.where(later, jnp.exp(jnp.minimum(gap, 0.0)), 0.0)
        decayed = decay * dot_nt(x, dy)
        pair_sum = pair_sum + decayed
        gx_ref[:, h * size : (h + 1) * size] = dot((decay * bct).astype(BF16), dy)
        reach = dot((decayed * bct).astype(BF16), at_or_after)
        inside_ref[h : h + 1, :] = jnp.sum(jnp.where(row < col, reach, 0.0), axis=0, keepdims=True)
    grad_ref[:steps] = dot(pair_sum.astype(BF16), c_rows)
    grad_ref[steps:] = dot(pair_sum.T.astype(BF16), b_rows)


def scan_kernel(parts_ref, out_ref):
    slabs, rows, _ = out_ref.shape
    rows -= EXTRA_ROWS
    half = rows // 2

    def extra(t, k):
        return parts_ref[t, rows + k : rows + k + 1, :]

    decays = [jnp.exp(extra(t, 0) + extra(t, 1) + extra(t, 2)) for t in range(slabs)]
    grads = [jnp.zeros((half, N), F32)]
    for t in range(slabs - 1, 0, -1):
        grads.append(decays[t] * grads[-1] + power(extra(t, 4)) * parts_ref[t, half:rows, :])
    grads = grads[::-1]
    state = jnp.zeros((half, N), F32)
    for t in range(slabs):
        out_ref[t, :half, :] = state.astype(BF16)
        out_ref[t, half:rows, :] = grads[t].astype(BF16)
        product = jnp.sum(state * grads[t], axis=0, keepdims=True)
        out_ref[t, rows:, :] = three_terms(product).astype(BF16)
        state = decays[t] * state + power(extra(t, 3)) * parts_ref[t, :half, :]


def entering(in_ref):
    parts, rows, _ = in_ref.shape
    half = (rows - EXTRA_ROWS) // 2
    state = in_ref[:, :half, :].reshape(parts * half, N)
    grad = in_ref[:, half : 2 * half, :].reshape(parts * half, N)
    return state, grad


def bc_grad_kernel(in_ref, xe_ref, dyf_ref, local_ref, out_ref):
    state, grad = entering(in_ref)
    steps = xe_ref.shape[0]
    out_ref[:N, :] = (local_ref[:steps] + dot(xe_ref[...], grad)).T.astype(BF16)
    out_ref[N:, :] = (local_ref[steps:] + dot(dyf_ref[...], state)).T.astype(BF16)


def finish_kernel(in_ref, own_ref, other_ref, x_ref, dy_ref, log_ref, logt_ref, gx_ref, inside_ref, out_ref, out_log_ref):
    state, grad = entering(in_ref)
    b_rows, c_rows = (rows.astype(BF16) for rows in whole_bc(own_ref, other_ref))
    steps, heads = log_ref.shape
    width = x_ref.shape[1]
    row, col = iotas(steps)
    cum, cumt = decay_sums(log_ref, logt_ref)
    to_end, from_start = decay_factors(cum, width)
    b_state = to_end * dot_nt(b_rows, grad)
    c_state = from_start * dot_nt(c_rows, state)
    out_ref[...] = gx_ref[...] + b_state
    spread = head_spread(heads, width)
    earlier = dot_nt(spread, c_state * dy_ref[...], HIGHEST)
    later = dot_nt(spread, b_state * x_ref[...], HIGHEST)
    parts = in_ref.shape[0]
    products = jnp.sum(in_ref[:, -EXTRA_ROWS:, :].astype(F32), axis=1)
    products = jnp.sum(products.reshape(heads, parts // heads, N), axis=1)
    across = jnp.sum(products, axis=1, keepdims=True)
    across = across * jnp.exp(cumt[:, steps - 1 : steps])
    out_log_ref[...] = (
        inside_ref[...]
        + dot(earlier, (row >= col).astype(F32), HIGHEST)
        + dot(later, (row < col).astype(F32), HIGHEST)
        + across
    )


def grad_input_kernel(core_ref, grads_ref, own_ref, other_ref, out_ref):
    first = core_ref[0] == 0
    groups = grads_ref.shape[0]
    total = jnp.zeros(out_ref.shape, F32)
    for group in range(groups):
        rows = blocks_of(first, own_ref, other_ref, group, groups // 2)
        total = total + dot_tn(grads_ref[group], rows)
    out_ref[...] = total.astype(BF16)


def row_blocks_kernel(grads_ref, out_ref):
    lines, _, rows, _ = out_ref.shape
    for group in range(grads_ref.shape[0]):
        column, high = divmod(group, 2)
        for k in range(2):
            for core in range(2):
                at = (2 * k + core) * rows
                out_ref[2 * high + k, 2 * column + core] = grads_ref[group, at : at + rows, :]


def grad_weight_kernel(place_ref, grads_ref, x0_ref, x1_ref, x2_ref, x3_ref, keep_ref, send_ref):
    first = place_ref[0] == 0
    line = place_ref[1]
    columns, rows, width = keep_ref.shape
    x = jnp.concatenate([ref[...] for ref in (x0_ref, x1_ref, x2_ref, x3_ref)], axis=0)
    for column in range(columns):
        grads = jnp.concatenate(
            [
                grads_ref[line ^ k, 2 * column : 2 * column + 2].reshape(2 * rows, -1)
                for k in range(grads_ref.shape[0])
            ],
            axis=1,
        )
        part = dot(grads, x)
        one, other = part[:rows], part[rows:]
        keep_ref[column] = jnp.where(first, one, other)
        send_ref[column] = jnp.where(first, other, one).astype(BF16)


def chip_sum_kernel(own_ref, other_ref, out_ref):
    for k in range(out_ref.shape[0]):
        out_ref[k] = (own_ref[k] + other_ref[k].astype(F32)).astype(BF16)


def line_sum_kernel(parts_ref, out_ref):
    total = parts_ref[0].astype(F32)
    for k in range(1, parts_ref.shape[0]):
        total = total + parts_ref[k].astype(F32)
    out_ref[...] = total


def copies_kernel(own_ref, other_ref, out_ref):
    total = (own_ref[...].astype(F32) + other_ref[...].astype(F32)).astype(BF16)
    for k in range(out_ref.shape[0]):
        out_ref[k] = total


def shape(dims, dtype=F32):
    return jax.ShapeDtypeStruct(dims, dtype)


def to_all(block, axis):
    count = lax.axis_size(axis)
    return lax.all_to_all(jnp.broadcast_to(block[None], (count,) + block.shape), axis, 0, 0)


def flip(block, axis, bit):
    return lax.ppermute(block, axis, [(k, k ^ bit) for k in range(lax.axis_size(axis))])


def swap(block, axis):
    return flip(block, axis, 1)


def on_device(layer_input, proj_weight, ssd_input, log_decay, out_grad):
    steps, width = layer_input.shape
    heads = log_decay.shape[1]
    slabs = lax.axis_size(TM)
    groups = lax.axis_size("z")
    rows_here = proj_weight.shape[0]
    core = lax.axis_index("core").reshape(1)
    share = ssd_input.shape[1] // slabs
    logt = log_decay.T

    line_w = to_all(proj_weight, "ylo")
    own_w = to_all(line_w, "x").reshape(-1, rows_here, width)
    other_w = swap(own_w, "core")
    xe, dyf, xet, dyft, ds = call(
        prepare,
        (
            shape(ssd_input.shape, BF16),
            shape(ssd_input.shape, BF16),
            shape(ssd_input.shape[::-1]),
            shape(ssd_input.shape[::-1]),
            shape((heads, N)),
        ),
        10**7,
        ssd_input,
        out_grad,
        log_decay,
        logt,
    )
    partial = call(
        partial_kernel,
        shape((groups, steps + EXTRA_ROWS, 2 * N)),
        2 * steps * width * slabs * rows_here,
        core,
        layer_input,
        own_w,
        other_w,
        smem=1,
    )
    pieces = lax.all_to_all(partial.astype(F16), "z", 0, 0).astype(F32)
    own_bc = call(sum_kernel, shape((steps + EXTRA_ROWS, 2 * N)), 10**6, pieces).astype(F16)
    other_bc = swap(own_bc, "yhi").astype(F32)
    own_bc = own_bc.astype(F32)

    parts = call(
        states_kernel,
        shape((slabs, 2 * share + EXTRA_ROWS, N)),
        12 * steps * N * ssd_input.shape[1],
        own_bc,
        other_bc,
        xet,
        dyft,
        ds,
    )
    shares = lax.all_to_all(parts.astype(F16), TM, 0, 0).astype(F32)
    gx, local_grad, inside = call(
        local_kernel,
        (
            shape(ssd_input.shape),
            shape((2 * steps, N)),
            shape((heads, steps)),
        ),
        10**8,
        own_bc,
        other_bc,
        ssd_input,
        out_grad,
        log_decay,
        logt,
    )
    carried = call(scan_kernel, shape(shares.shape, BF16), 10**6, shares)
    arrived = lax.all_to_all(carried, TM, 0, 0)
    own_grad = call(
        bc_grad_kernel,
        shape((2 * N, steps), BF16),
        4 * steps * N * ssd_input.shape[1],
        arrived,
        xe,
        dyf,
        local_grad,
    )
    other_grad = swap(own_grad, "yhi")
    grad_x, grad_log = call(
        finish_kernel,
        (shape(ssd_input.shape), shape((heads, steps))),
        10**8,
        arrived,
        own_bc,
        other_bc,
        ssd_input,
        out_grad,
        log_decay,
        logt,
        gx,
        inside,
    )
    copies = call(copies_kernel, shape((groups, 2 * N, steps), BF16), 10**6, own_grad, other_grad)
    all_grads = lax.all_to_all(copies, "z", 0, 0)
    late_input, _ = lax.optimization_barrier((layer_input, copies))
    near = flip(late_input, "x", 1)
    x_along = (near, flip(late_input, "x", 2), flip(near, "x", 2))
    all_grads, x_along, grad_x, grad_log = lax.optimization_barrier(
        (all_grads, x_along, grad_x, grad_log)
    )

    columns = groups // 2
    blocks = call(
        row_blocks_kernel, shape((4, 2 * columns, rows_here, steps), BF16), 10**6, all_grads
    )
    row_grads = lax.all_to_all(blocks, "x", 0, 0)
    grad_input = call(
        grad_input_kernel,
        shape(layer_input.shape, BF16),
        2 * steps * width * slabs * rows_here,
        core,
        all_grads,
        own_w,
        other_w,
        smem=1,
    )
    row_grads, grad_input = lax.optimization_barrier((row_grads, grad_input))
    keep, send = call(
        grad_weight_kernel,
        (shape((columns, rows_here, width)), shape((columns, rows_here, width), BF16)),
        2 * steps * width * slabs * rows_here,
        jnp.concatenate([core, lax.axis_index("x").reshape(1)]),
        row_grads,
        layer_input,
        *x_along,
        smem=1,
    )
    of_chip = call(chip_sum_kernel, shape(send.shape, BF16), 10**6, keep, swap(send, "core"))
    of_line = lax.all_to_all(of_chip, "ylo", 0, 0)
    grad_weight = call(line_sum_kernel, shape(proj_weight.shape), 10**6, of_line)
    return grad_x, grad_log.T, grad_input, grad_weight


def solution(mesh):
    fine = Mesh(mesh.devices.reshape(4, 4, 2, 8, 2), TM + HEADS)
    spec = P(TM, HEADS)
    return jax.shard_map(
        on_device,
        mesh=fine,
        in_specs=(spec,) * 5,
        out_specs=(spec,) * 4,
        check_vma=False,
    )
```

```python
import jax
import jax.numpy as jnp
from jax import lax
from jax.experimental import pallas as pl
from jax.experimental.pallas import tpu as pltpu
from jax.sharding import Mesh
from jax.sharding import PartitionSpec as P

N = 128
EXTRA_ROWS = 8
LN2 = 0.6931471805599453
F32 = jnp.float32
BF16 = jnp.bfloat16
F16 = jnp.float16
HIGHEST = lax.Precision.HIGHEST
TM = ("ylo", "x", "core")
HEADS = ("z", "yhi")


def dot(a, b, precision=None):
    return jnp.dot(a, b, preferred_element_type=F32, precision=precision)


def dot_nt(a, b, precision=None):
    return lax.dot_general(
        a, b, (((1,), (1,)), ((), ())), preferred_element_type=F32, precision=precision
    )


def dot_tn(a, b):
    return lax.dot_general(a, b, (((0,), (0,)), ((), ())), preferred_element_type=F32)


def split(a):
    high = a.astype(BF16)
    return high, (a - high.astype(F32)).astype(BF16)


def dot_split(a, b):
    a_high, a_low = split(a)
    b_high, b_low = split(b)
    return dot(a_high, b_high) + dot(a_low, b_high) + dot(a_high, b_low)


def three_terms(row):
    high = row.astype(BF16).astype(F32)
    middle = (row - high).astype(BF16).astype(F32)
    low = row - high - middle
    term = lax.broadcasted_iota(jnp.int32, (EXTRA_ROWS, N), 0)
    return jnp.where(
        term == 0, high, jnp.where(term == 1, middle, jnp.where(term == 2, low, 0.0))
    )


def exponent_of(a):
    top = jnp.max(jnp.max(jnp.abs(a), axis=1, keepdims=True), axis=0, keepdims=True)
    return jnp.ceil(jnp.log(jnp.maximum(top, 1e-30)) * (1.0 / LN2)) - 14.0


def power(exponent):
    return jnp.exp(exponent * LN2)


def iotas(n):
    return (
        lax.broadcasted_iota(jnp.int32, (n, n), 0),
        lax.broadcasted_iota(jnp.int32, (n, n), 1),
    )


def head_spread(heads, width):
    size = width // heads
    row = lax.broadcasted_iota(jnp.int32, (heads, width), 0)
    col = lax.broadcasted_iota(jnp.int32, (heads, width), 1)
    return ((col >= row * size) & (col < (row + 1) * size)).astype(F32)


def call(kernel, outs, flops, *args, smem=0):
    out_list = outs if isinstance(outs, tuple) else (outs,)
    read = sum(a.size * a.dtype.itemsize for a in args)
    wrote = sum(o.size * o.dtype.itemsize for o in out_list)
    spaces = [pltpu.SMEM if k < smem else pltpu.VMEM for k in range(len(args))]
    return pl.pallas_call(
        kernel,
        out_shape=outs,
        in_specs=[pl.BlockSpec(memory_space=space) for space in spaces],
        out_specs=jax.tree.map(lambda _: pl.BlockSpec(memory_space=pltpu.VMEM), outs),
        cost_estimate=pl.CostEstimate(
            flops=flops, bytes_accessed=read + wrote, transcendentals=0
        ),
        compiler_params=pltpu.CompilerParams(vmem_limit_bytes=16 * 2**20),
    )(*args)


def decay_sums(log_ref, logt_ref):
    row, col = iotas(log_ref.shape[0])
    cum = dot((row >= col).astype(F32), log_ref[...], HIGHEST)
    cumt = dot(logt_ref[...], (row <= col).astype(F32), HIGHEST)
    return cum, cumt


def decay_factors(cum, width):
    spread = head_spread(cum.shape[1], width)
    last = cum[cum.shape[0] - 1 :, :]
    return dot(jnp.exp(last - cum), spread, HIGHEST), dot(jnp.exp(cum), spread, HIGHEST)


def prepare(x_ref, dy_ref, log_ref, logt_ref, xet_ref, dyft_ref, ds_ref):
    steps = log_ref.shape[0]
    cum, cumt = decay_sums(log_ref, logt_ref)
    to_end, from_start = decay_factors(cum, x_ref.shape[1])
    xet_ref[...] = (x_ref[...] * to_end).T
    dyft_ref[...] = (dy_ref[...] * from_start).T
    ds_ref[...] = jnp.broadcast_to(cumt[:, steps - 1 : steps], ds_ref.shape)


def blocks_of(first, own_ref, other_ref, group, lines):
    column, half = divmod(group, 2)
    rows = []
    for line in (2 * half, 2 * half + 1):
        at = line * lines + column
        own, other = own_ref[at], other_ref[at]
        rows += [jnp.where(first, own, other), jnp.where(first, other, own)]
    return jnp.concatenate(rows, axis=0)


def partial_kernel(core_ref, x_ref, own_ref, other_ref, out_ref):
    first = core_ref[0] == 0
    x = x_ref[...]
    steps = x.shape[0]
    groups, _, columns = out_ref.shape
    top = jnp.zeros((steps, columns), F32)
    for group in range(groups):
        part = dot_nt(x, blocks_of(first, own_ref, other_ref, group, groups // 2))
        top = jnp.maximum(top, jnp.abs(part))
        out_ref[group, :steps, :] = part
    exponent = exponent_of(top)
    scale = power(-exponent)
    for group in range(groups):
        out_ref[group, :steps, :] = out_ref[group, :steps, :] * scale
        out_ref[group, steps:, :] = jnp.broadcast_to(exponent, (EXTRA_ROWS, columns))


def sum_kernel(pieces_ref, out_ref):
    pieces, rows, columns = pieces_ref.shape
    steps = rows - EXTRA_ROWS
    exponents = [pieces_ref[k, steps:, :] for k in range(pieces)]
    top = exponents[0]
    for exponent in exponents[1:]:
        top = jnp.maximum(top, exponent)
    top = top + jnp.ceil(jnp.log(1.0 * pieces) / LN2)
    total = jnp.zeros((steps, columns), F32)
    for k in range(pieces):
        total = total + pieces_ref[k, :steps, :] * power(exponents[k] - top)[:1, :]
    out_ref[:steps, :] = total
    out_ref[steps:, :] = top


def whole_bc(own_ref, other_ref):
    steps = own_ref.shape[0] - EXTRA_ROWS
    bc = own_ref[:steps, :] * power(own_ref[steps : steps + 1, :])
    bc = bc + other_ref[:steps, :] * power(other_ref[steps : steps + 1, :])
    return bc[:, :N], bc[:, N:]


def states_kernel(own_ref, other_ref, xet_ref, dyft_ref, ds_ref, out_ref):
    b_rows, c_rows = whole_bc(own_ref, other_ref)
    heads = ds_ref.shape[0]
    parts, rows, _ = out_ref.shape
    half = (rows - EXTRA_ROWS) // 2
    state = dot_split(xet_ref[...], b_rows)
    grad = dot_split(dyft_ref[...], c_rows)
    state_exponent = exponent_of(state)
    grad_exponent = exponent_of(grad)
    out_ref[:, :half, :] = (state * power(-state_exponent)).reshape(parts, half, N)
    out_ref[:, half : 2 * half, :] = (grad * power(-grad_exponent)).reshape(parts, half, N)
    row = lax.broadcasted_iota(jnp.int32, (EXTRA_ROWS, N), 0)
    for head in range(heads):
        terms = jnp.where(row == 3, state_exponent, three_terms(ds_ref[head : head + 1, :]))
        terms = jnp.where(row == 4, grad_exponent, terms)
        for part in range(head * parts // heads, (head + 1) * parts // heads):
            out_ref[part, 2 * half :, :] = terms


def local_kernel(own_ref, other_ref, x_ref, dy_ref, log_ref, logt_ref, gx_ref, terms_ref, inside_ref):
    b_rows, c_rows = (rows.astype(BF16) for rows in whole_bc(own_ref, other_ref))
    steps, heads = log_ref.shape
    size = x_ref.shape[1] // heads
    row, col = iotas(steps)
    later = row <= col
    at_or_after = (row >= col).astype(BF16)
    bct = dot_nt(b_rows, c_rows)
    pair_sum = jnp.zeros((steps, steps), F32)
    cum, cumt = decay_sums(log_ref, logt_ref)
    for h in range(heads):
        x = x_ref[:, h * size : (h + 1) * size].astype(BF16)
        dy = dy_ref[:, h * size : (h + 1) * size].astype(BF16)
        gap = cumt[h : h + 1, :] - cum[:, h : h + 1]
        decay = jnp.where(later, jnp.exp(jnp.minimum(gap, 0.0)), 0.0)
        decayed = decay * dot_nt(x, dy)
        pair_sum = pair_sum + decayed
        gx_ref[:, h * size : (h + 1) * size] = dot((decay * bct).astype(BF16), dy)
        reach = dot((decayed * bct).astype(BF16), at_or_after)
        inside_ref[h : h + 1, :] = jnp.sum(jnp.where(row < col, reach, 0.0), axis=0, keepdims=True)
    width = x_ref.shape[1]
    to_end, from_start = decay_factors(cum, width)
    terms_ref[:, :width] = x_ref[...] * to_end
    terms_ref[:, width : 2 * width] = dy_ref[...] * from_start
    terms_ref[:, 2 * width : 2 * width + N] = dot(pair_sum.astype(BF16), c_rows)
    terms_ref[:, 2 * width + N :] = dot(pair_sum.T.astype(BF16), b_rows)


def scan_kernel(parts_ref, out_ref):
    slabs, rows, _ = out_ref.shape
    rows -= EXTRA_ROWS
    half = rows // 2

    def extra(t, k):
        return parts_ref[t, rows + k : rows + k + 1, :]

    decays = [jnp.exp(extra(t, 0) + extra(t, 1) + extra(t, 2)) for t in range(slabs)]
    grads = [jnp.zeros((half, N), F32)]
    for t in range(slabs - 1, 0, -1):
        grads.append(decays[t] * grads[-1] + power(extra(t, 4)) * parts_ref[t, half:rows, :])
    grads = grads[::-1]
    state = jnp.zeros((half, N), F32)
    for t in range(slabs):
        out_ref[t, :half, :] = state.astype(BF16)
        out_ref[t, half:rows, :] = grads[t].astype(BF16)
        product = jnp.sum(state * grads[t], axis=0, keepdims=True)
        out_ref[t, rows:, :] = three_terms(product).astype(BF16)
        state = decays[t] * state + power(extra(t, 3)) * parts_ref[t, :half, :]


def entering(in_ref):
    parts, rows, _ = in_ref.shape
    half = (rows - EXTRA_ROWS) // 2
    state = in_ref[:, :half, :].reshape(parts * half, N)
    grad = in_ref[:, half : 2 * half, :].reshape(parts * half, N)
    return state, grad


def bc_grad_kernel(in_ref, terms_ref, out_ref):
    state, grad = entering(in_ref)
    width = state.shape[0]
    from_grad = dot(terms_ref[:, :width].astype(BF16), grad)
    from_state = dot(terms_ref[:, width : 2 * width].astype(BF16), state)
    out_ref[:N, :] = (terms_ref[:, 2 * width : 2 * width + N] + from_grad).T.astype(BF16)
    out_ref[N:, :] = (terms_ref[:, 2 * width + N :] + from_state).T.astype(BF16)


def finish_kernel(in_ref, own_ref, other_ref, x_ref, dy_ref, log_ref, logt_ref, gx_ref, inside_ref, out_ref, out_log_ref):
    state, grad = entering(in_ref)
    b_rows, c_rows = (rows.astype(BF16) for rows in whole_bc(own_ref, other_ref))
    steps, heads = log_ref.shape
    width = x_ref.shape[1]
    row, col = iotas(steps)
    cum, cumt = decay_sums(log_ref, logt_ref)
    to_end, from_start = decay_factors(cum, width)
    b_state = to_end * dot_nt(b_rows, grad)
    c_state = from_start * dot_nt(c_rows, state)
    out_ref[...] = gx_ref[...] + b_state
    spread = head_spread(heads, width)
    earlier = dot_nt(spread, c_state * dy_ref[...], HIGHEST)
    later = dot_nt(spread, b_state * x_ref[...], HIGHEST)
    parts = in_ref.shape[0]
    products = jnp.sum(in_ref[:, -EXTRA_ROWS:, :].astype(F32), axis=1)
    products = jnp.sum(products.reshape(heads, parts // heads, N), axis=1)
    across = jnp.sum(products, axis=1, keepdims=True)
    across = across * jnp.exp(cumt[:, steps - 1 : steps])
    out_log_ref[...] = (
        inside_ref[...]
        + dot(earlier, (row >= col).astype(F32), HIGHEST)
        + dot(later, (row < col).astype(F32), HIGHEST)
        + across
    )


def grad_input_kernel(core_ref, grads_ref, own_ref, other_ref, out_ref):
    first = core_ref[0] == 0
    groups = grads_ref.shape[0]
    total = jnp.zeros(out_ref.shape, F32)
    for group in range(groups):
        rows = blocks_of(first, own_ref, other_ref, group, groups // 2)
        total = total + dot_tn(grads_ref[group], rows)
    out_ref[...] = total.astype(BF16)


def row_blocks_kernel(grads_ref, out_ref):
    lines, _, rows, _ = out_ref.shape
    for group in range(grads_ref.shape[0]):
        column, high = divmod(group, 2)
        for k in range(2):
            for core in range(2):
                at = (2 * k + core) * rows
                out_ref[2 * high + k, 2 * column + core] = grads_ref[group, at : at + rows, :]


def stack_kernel(x0_ref, x1_ref, x2_ref, x3_ref, out_ref):
    steps = x0_ref.shape[0]
    for k, ref in enumerate((x0_ref, x1_ref, x2_ref, x3_ref)):
        out_ref[k * steps : (k + 1) * steps, :] = ref[...]


def grad_weight_kernel(place_ref, grads_ref, x_ref, keep_ref, send_ref):
    first = place_ref[0] == 0
    line = place_ref[1]
    columns, rows, width = keep_ref.shape
    x = x_ref[...]
    for column in range(columns):
        grads = jnp.concatenate(
            [
                grads_ref[line ^ k, 2 * column : 2 * column + 2].reshape(2 * rows, -1)
                for k in range(grads_ref.shape[0])
            ],
            axis=1,
        )
        part = dot(grads, x)
        one, other = part[:rows], part[rows:]
        keep_ref[column] = jnp.where(first, one, other)
        send_ref[column] = jnp.where(first, other, one).astype(BF16)


def chip_sum_kernel(own_ref, other_ref, out_ref):
    for k in range(out_ref.shape[0]):
        out_ref[k] = (own_ref[k] + other_ref[k].astype(F32)).astype(BF16)


def line_sum_kernel(parts_ref, out_ref):
    total = parts_ref[0].astype(F32)
    for k in range(1, parts_ref.shape[0]):
        total = total + parts_ref[k].astype(F32)
    out_ref[...] = total


def copies_kernel(own_ref, other_ref, out_ref):
    total = (own_ref[...].astype(F32) + other_ref[...].astype(F32)).astype(BF16)
    for k in range(out_ref.shape[0]):
        out_ref[k] = total


def shape(dims, dtype=F32):
    return jax.ShapeDtypeStruct(dims, dtype)


def to_all(block, axis):
    count = lax.axis_size(axis)
    return lax.all_to_all(jnp.broadcast_to(block[None], (count,) + block.shape), axis, 0, 0)


def flip(block, axis, bit):
    return lax.ppermute(block, axis, [(k, k ^ bit) for k in range(lax.axis_size(axis))])


def swap(block, axis):
    return flip(block, axis, 1)


def on_device(layer_input, proj_weight, ssd_input, log_decay, out_grad):
    steps, width = layer_input.shape
    heads = log_decay.shape[1]
    slabs = lax.axis_size(TM)
    groups = lax.axis_size("z")
    rows_here = proj_weight.shape[0]
    core = lax.axis_index("core").reshape(1)
    share = ssd_input.shape[1] // slabs
    logt = log_decay.T

    line_w = to_all(proj_weight, "ylo")
    own_w = to_all(line_w, "x").reshape(-1, rows_here, width)
    other_w = swap(own_w, "core")
    xet, dyft, ds = call(
        prepare,
        (
            shape(ssd_input.shape[::-1]),
            shape(ssd_input.shape[::-1]),
            shape((heads, N)),
        ),
        10**7,
        ssd_input,
        out_grad,
        log_decay,
        logt,
    )
    partial = call(
        partial_kernel,
        shape((groups, steps + EXTRA_ROWS, 2 * N)),
        2 * steps * width * slabs * rows_here,
        core,
        layer_input,
        own_w,
        other_w,
        smem=1,
    )
    pieces = lax.all_to_all(partial.astype(F16), "z", 0, 0).astype(F32)
    own_bc = call(sum_kernel, shape((steps + EXTRA_ROWS, 2 * N)), 10**6, pieces).astype(F16)
    other_bc = swap(own_bc, "yhi").astype(F32)
    own_bc = own_bc.astype(F32)

    parts = call(
        states_kernel,
        shape((slabs, 2 * share + EXTRA_ROWS, N)),
        12 * steps * N * ssd_input.shape[1],
        own_bc,
        other_bc,
        xet,
        dyft,
        ds,
    )
    shares = lax.all_to_all(parts.astype(F16), TM, 0, 0).astype(F32)
    gx, terms, inside = call(
        local_kernel,
        (
            shape(ssd_input.shape),
            shape((steps, 2 * (ssd_input.shape[1] + N))),
            shape((heads, steps)),
        ),
        10**8,
        own_bc,
        other_bc,
        ssd_input,
        out_grad,
        log_decay,
        logt,
    )
    carried = call(scan_kernel, shape(shares.shape, BF16), 10**6, shares)
    arrived = lax.all_to_all(carried, TM, 0, 0)
    own_grad = call(
        bc_grad_kernel,
        shape((2 * N, steps), BF16),
        4 * steps * N * ssd_input.shape[1],
        arrived,
        terms,
    )
    other_grad = swap(own_grad, "yhi")
    grad_x, grad_log = call(
        finish_kernel,
        (shape(ssd_input.shape), shape((heads, steps))),
        10**8,
        arrived,
        own_bc,
        other_bc,
        ssd_input,
        out_grad,
        log_decay,
        logt,
        gx,
        inside,
    )
    other_grad, grad_x, grad_log = lax.optimization_barrier((other_grad, grad_x, grad_log))
    copies = call(copies_kernel, shape((groups, 2 * N, steps), BF16), 10**6, own_grad, other_grad)
    all_grads = lax.all_to_all(copies, "z", 0, 0)
    late_input, _ = lax.optimization_barrier((layer_input, copies))
    near = flip(late_input, "x", 1)
    x_along = call(
        stack_kernel,
        shape((4 * steps, width), BF16),
        10**6,
        late_input,
        near,
        flip(late_input, "x", 2),
        flip(near, "x", 2),
    )
    all_grads, x_along = lax.optimization_barrier((all_grads, x_along))

    columns = groups // 2
    blocks = call(
        row_blocks_kernel, shape((4, 2 * columns, rows_here, steps), BF16), 10**6, all_grads
    )
    row_grads = lax.all_to_all(blocks, "x", 0, 0)
    grad_input = call(
        grad_input_kernel,
        shape(layer_input.shape, BF16),
        2 * steps * width * slabs * rows_here,
        core,
        all_grads,
        own_w,
        other_w,
        smem=1,
    )
    row_grads, grad_input = lax.optimization_barrier((row_grads, grad_input))
    keep, send = call(
        grad_weight_kernel,
        (shape((columns, rows_here, width)), shape((columns, rows_here, width), BF16)),
        2 * steps * width * slabs * rows_here,
        jnp.concatenate([core, lax.axis_index("x").reshape(1)]),
        row_grads,
        x_along,
        smem=1,
    )
    of_chip = call(chip_sum_kernel, shape(send.shape, BF16), 10**6, keep, swap(send, "core"))
    of_line = lax.all_to_all(of_chip, "ylo", 0, 0)
    grad_weight = call(line_sum_kernel, shape(proj_weight.shape), 10**6, of_line)
    return grad_x, grad_log.T, grad_input, grad_weight


def solution(mesh):
    fine = Mesh(mesh.devices.reshape(4, 4, 2, 8, 2), TM + HEADS)
    spec = P(TM, HEADS)
    return jax.shard_map(
        on_device,
        mesh=fine,
        in_specs=(spec,) * 5,
        out_specs=(spec,) * 4,
        check_vma=False,
    )
```

```python
import jax
import jax.numpy as jnp
from jax import lax
from jax.experimental import pallas as pl
from jax.experimental.pallas import tpu as pltpu
from jax.sharding import Mesh
from jax.sharding import PartitionSpec as P

N = 128
EXTRA_ROWS = 8
LN2 = 0.6931471805599453
F32 = jnp.float32
BF16 = jnp.bfloat16
F16 = jnp.float16
HIGHEST = lax.Precision.HIGHEST
TM = ("ylo", "x", "core")
HEADS = ("z", "yhi")


def dot(a, b, precision=None):
    return jnp.dot(a, b, preferred_element_type=F32, precision=precision)


def dot_nt(a, b, precision=None):
    return lax.dot_general(
        a, b, (((1,), (1,)), ((), ())), preferred_element_type=F32, precision=precision
    )


def dot_tn(a, b):
    return lax.dot_general(a, b, (((0,), (0,)), ((), ())), preferred_element_type=F32)


def split(a):
    high = a.astype(BF16)
    return high, (a - high.astype(F32)).astype(BF16)


def dot_split(a, b):
    a_high, a_low = split(a)
    b_high, b_low = split(b)
    return dot(a_high, b_high) + dot(a_low, b_high) + dot(a_high, b_low)


def three_terms(row):
    high = row.astype(BF16).astype(F32)
    middle = (row - high).astype(BF16).astype(F32)
    low = row - high - middle
    term = lax.broadcasted_iota(jnp.int32, (EXTRA_ROWS, N), 0)
    return jnp.where(
        term == 0, high, jnp.where(term == 1, middle, jnp.where(term == 2, low, 0.0))
    )


def exponent_of(a):
    top = jnp.max(jnp.max(jnp.abs(a), axis=1, keepdims=True), axis=0, keepdims=True)
    return jnp.ceil(jnp.log(jnp.maximum(top, 1e-30)) * (1.0 / LN2)) - 14.0


def power(exponent):
    return jnp.exp(exponent * LN2)


def iotas(n):
    return (
        lax.broadcasted_iota(jnp.int32, (n, n), 0),
        lax.broadcasted_iota(jnp.int32, (n, n), 1),
    )


def head_spread(heads, width):
    size = width // heads
    row = lax.broadcasted_iota(jnp.int32, (heads, width), 0)
    col = lax.broadcasted_iota(jnp.int32, (heads, width), 1)
    return ((col >= row * size) & (col < (row + 1) * size)).astype(F32)


def call(kernel, outs, flops, *args, smem=0):
    out_list = outs if isinstance(outs, tuple) else (outs,)
    read = sum(a.size * a.dtype.itemsize for a in args)
    wrote = sum(o.size * o.dtype.itemsize for o in out_list)
    spaces = [pltpu.SMEM if k < smem else pltpu.VMEM for k in range(len(args))]
    return pl.pallas_call(
        kernel,
        out_shape=outs,
        in_specs=[pl.BlockSpec(memory_space=space) for space in spaces],
        out_specs=jax.tree.map(lambda _: pl.BlockSpec(memory_space=pltpu.VMEM), outs),
        cost_estimate=pl.CostEstimate(
            flops=flops, bytes_accessed=read + wrote, transcendentals=0
        ),
        compiler_params=pltpu.CompilerParams(vmem_limit_bytes=16 * 2**20),
    )(*args)


def decay_sums(log_ref, logt_ref):
    row, col = iotas(log_ref.shape[0])
    cum = dot((row >= col).astype(F32), log_ref[...], HIGHEST)
    cumt = dot(logt_ref[...], (row <= col).astype(F32), HIGHEST)
    return cum, cumt


def decay_factors(cum, width):
    spread = head_spread(cum.shape[1], width)
    last = cum[cum.shape[0] - 1 :, :]
    return dot(jnp.exp(last - cum), spread, HIGHEST), dot(jnp.exp(cum), spread, HIGHEST)


def prepare(x_ref, dy_ref, log_ref, logt_ref, xet_ref, dyft_ref, ds_ref):
    steps = log_ref.shape[0]
    cum, cumt = decay_sums(log_ref, logt_ref)
    to_end, from_start = decay_factors(cum, x_ref.shape[1])
    xet_ref[...] = (x_ref[...] * to_end).T
    dyft_ref[...] = (dy_ref[...] * from_start).T
    ds_ref[...] = jnp.broadcast_to(cumt[:, steps - 1 : steps], ds_ref.shape)


def blocks_of(first, own_ref, other_ref, group, lines):
    column, half = divmod(group, 2)
    rows = []
    for line in (2 * half, 2 * half + 1):
        at = line * lines + column
        own, other = own_ref[at], other_ref[at]
        rows += [jnp.where(first, own, other), jnp.where(first, other, own)]
    return jnp.concatenate(rows, axis=0)


def partial_kernel(core_ref, x_ref, own_ref, other_ref, out_ref):
    first = core_ref[0] == 0
    x = x_ref[...]
    steps = x.shape[0]
    groups, _, columns = out_ref.shape
    top = jnp.zeros((steps, columns), F32)
    for group in range(groups):
        part = dot_nt(x, blocks_of(first, own_ref, other_ref, group, groups // 2))
        top = jnp.maximum(top, jnp.abs(part))
        out_ref[group, :steps, :] = part
    exponent = exponent_of(top)
    scale = power(-exponent)
    for group in range(groups):
        out_ref[group, :steps, :] = out_ref[group, :steps, :] * scale
        out_ref[group, steps:, :] = jnp.broadcast_to(exponent, (EXTRA_ROWS, columns))


def sum_kernel(pieces_ref, out_ref):
    pieces, rows, columns = pieces_ref.shape
    steps = rows - EXTRA_ROWS
    exponents = [pieces_ref[k, steps:, :] for k in range(pieces)]
    top = exponents[0]
    for exponent in exponents[1:]:
        top = jnp.maximum(top, exponent)
    top = top + jnp.ceil(jnp.log(1.0 * pieces) / LN2)
    total = jnp.zeros((steps, columns), F32)
    for k in range(pieces):
        total = total + pieces_ref[k, :steps, :] * power(exponents[k] - top)[:1, :]
    out_ref[:steps, :] = total
    out_ref[steps:, :] = top


def whole_bc(halves_ref):
    steps = halves_ref.shape[1] - EXTRA_ROWS
    bc = sum(
        halves_ref[k, :steps, :] * power(halves_ref[k, steps : steps + 1, :]) for k in range(2)
    )
    return bc[:, :N], bc[:, N:]


def states_kernel(halves_ref, xet_ref, dyft_ref, ds_ref, out_ref):
    b_rows, c_rows = whole_bc(halves_ref)
    heads = ds_ref.shape[0]
    parts, rows, _ = out_ref.shape
    half = (rows - EXTRA_ROWS) // 2
    state = dot_split(xet_ref[...], b_rows)
    grad = dot_split(dyft_ref[...], c_rows)
    state_exponent = exponent_of(state)
    grad_exponent = exponent_of(grad)
    out_ref[:, :half, :] = (state * power(-state_exponent)).reshape(parts, half, N)
    out_ref[:, half : 2 * half, :] = (grad * power(-grad_exponent)).reshape(parts, half, N)
    row = lax.broadcasted_iota(jnp.int32, (EXTRA_ROWS, N), 0)
    for head in range(heads):
        terms = jnp.where(row == 3, state_exponent, three_terms(ds_ref[head : head + 1, :]))
        terms = jnp.where(row == 4, grad_exponent, terms)
        for part in range(head * parts // heads, (head + 1) * parts // heads):
            out_ref[part, 2 * half :, :] = terms


def local_kernel(halves_ref, x_ref, dy_ref, log_ref, logt_ref, gx_ref, terms_ref, inside_ref):
    b_rows, c_rows = (rows.astype(BF16) for rows in whole_bc(halves_ref))
    steps, heads = log_ref.shape
    size = x_ref.shape[1] // heads
    row, col = iotas(steps)
    later = row <= col
    at_or_after = (row >= col).astype(BF16)
    bct = dot_nt(b_rows, c_rows)
    pair_sum = jnp.zeros((steps, steps), F32)
    cum, cumt = decay_sums(log_ref, logt_ref)
    for h in range(heads):
        x = x_ref[:, h * size : (h + 1) * size].astype(BF16)
        dy = dy_ref[:, h * size : (h + 1) * size].astype(BF16)
        gap = cumt[h : h + 1, :] - cum[:, h : h + 1]
        decay = jnp.where(later, jnp.exp(jnp.minimum(gap, 0.0)), 0.0)
        decayed = decay * dot_nt(x, dy)
        pair_sum = pair_sum + decayed
        gx_ref[:, h * size : (h + 1) * size] = dot((decay * bct).astype(BF16), dy)
        reach = dot((decayed * bct).astype(BF16), at_or_after)
        inside_ref[h : h + 1, :] = jnp.sum(jnp.where(row < col, reach, 0.0), axis=0, keepdims=True)
    width = x_ref.shape[1]
    to_end, from_start = decay_factors(cum, width)
    terms_ref[:, :width] = x_ref[...] * to_end
    terms_ref[:, width : 2 * width] = dy_ref[...] * from_start
    terms_ref[:, 2 * width : 2 * width + N] = dot(pair_sum.astype(BF16), c_rows)
    terms_ref[:, 2 * width + N :] = dot(pair_sum.T.astype(BF16), b_rows)


def scan_kernel(parts_ref, out_ref):
    slabs, rows, _ = out_ref.shape
    rows -= EXTRA_ROWS
    half = rows // 2

    def extra(t, k):
        return parts_ref[t, rows + k : rows + k + 1, :]

    decays = [jnp.exp(extra(t, 0) + extra(t, 1) + extra(t, 2)) for t in range(slabs)]
    grads = [jnp.zeros((half, N), F32)]
    for t in range(slabs - 1, 0, -1):
        grads.append(decays[t] * grads[-1] + power(extra(t, 4)) * parts_ref[t, half:rows, :])
    grads = grads[::-1]
    state = jnp.zeros((half, N), F32)
    for t in range(slabs):
        out_ref[t, :half, :] = state.astype(BF16)
        out_ref[t, half:rows, :] = grads[t].astype(BF16)
        product = jnp.sum(state * grads[t], axis=0, keepdims=True)
        out_ref[t, rows:, :] = three_terms(product).astype(BF16)
        state = decays[t] * state + power(extra(t, 3)) * parts_ref[t, :half, :]


def entering(in_ref):
    parts, rows, _ = in_ref.shape
    half = (rows - EXTRA_ROWS) // 2
    state = in_ref[:, :half, :].reshape(parts * half, N)
    grad = in_ref[:, half : 2 * half, :].reshape(parts * half, N)
    return state, grad


def bc_grad_kernel(in_ref, terms_ref, out_ref):
    state, grad = entering(in_ref)
    width = state.shape[0]
    from_grad = dot(terms_ref[:, :width].astype(BF16), grad)
    from_state = dot(terms_ref[:, width : 2 * width].astype(BF16), state)
    out_ref[:N, :] = (terms_ref[:, 2 * width : 2 * width + N] + from_grad).T.astype(BF16)
    out_ref[N:, :] = (terms_ref[:, 2 * width + N :] + from_state).T.astype(BF16)


def finish_kernel(in_ref, halves_ref, x_ref, dy_ref, log_ref, logt_ref, gx_ref, inside_ref, out_ref, out_log_ref):
    state, grad = entering(in_ref)
    b_rows, c_rows = (rows.astype(BF16) for rows in whole_bc(halves_ref))
    steps, heads = log_ref.shape
    width = x_ref.shape[1]
    row, col = iotas(steps)
    cum, cumt = decay_sums(log_ref, logt_ref)
    to_end, from_start = decay_factors(cum, width)
    b_state = to_end * dot_nt(b_rows, grad)
    c_state = from_start * dot_nt(c_rows, state)
    out_ref[...] = gx_ref[...] + b_state
    spread = head_spread(heads, width)
    earlier = dot_nt(spread, c_state * dy_ref[...], HIGHEST)
    later = dot_nt(spread, b_state * x_ref[...], HIGHEST)
    parts = in_ref.shape[0]
    products = jnp.sum(in_ref[:, -EXTRA_ROWS:, :].astype(F32), axis=1)
    products = jnp.sum(products.reshape(heads, parts // heads, N), axis=1)
    across = jnp.sum(products, axis=1, keepdims=True)
    across = across * jnp.exp(cumt[:, steps - 1 : steps])
    out_log_ref[...] = (
        inside_ref[...]
        + dot(earlier, (row >= col).astype(F32), HIGHEST)
        + dot(later, (row < col).astype(F32), HIGHEST)
        + across
    )


def grad_input_kernel(core_ref, grads_ref, own_ref, other_ref, out_ref):
    first = core_ref[0] == 0
    groups = grads_ref.shape[0]
    total = jnp.zeros(out_ref.shape, F32)
    for group in range(groups):
        rows = blocks_of(first, own_ref, other_ref, group, groups // 2)
        total = total + dot_tn(grads_ref[group], rows)
    out_ref[...] = total.astype(BF16)


def row_blocks_kernel(grads_ref, out_ref):
    lines, _, rows, _ = out_ref.shape
    for group in range(grads_ref.shape[0]):
        column, high = divmod(group, 2)
        for k in range(2):
            for core in range(2):
                at = (2 * k + core) * rows
                out_ref[2 * high + k, 2 * column + core] = grads_ref[group, at : at + rows, :]


def grad_weight_kernel(place_ref, grads_ref, low_ref, high_ref, keep_ref, send_ref):
    first = place_ref[0] == 0
    line = place_ref[1]
    columns, rows, width = keep_ref.shape
    x = jnp.concatenate([low_ref[...], high_ref[...]], axis=0)
    for column in range(columns):
        grads = jnp.concatenate(
            [
                grads_ref[line ^ k, 2 * column : 2 * column + 2].reshape(2 * rows, -1)
                for k in range(grads_ref.shape[0])
            ],
            axis=1,
        )
        part = dot(grads, x)
        one, other = part[:rows], part[rows:]
        keep_ref[column] = jnp.where(first, one, other)
        send_ref[column] = jnp.where(first, other, one).astype(BF16)


def chip_sum_kernel(own_ref, other_ref, out_ref):
    for k in range(out_ref.shape[0]):
        out_ref[k] = (own_ref[k] + other_ref[k].astype(F32)).astype(BF16)


def line_sum_kernel(parts_ref, out_ref):
    total = parts_ref[0].astype(F32)
    for k in range(1, parts_ref.shape[0]):
        total = total + parts_ref[k].astype(F32)
    out_ref[...] = total


def copies_kernel(halves_ref, out_ref):
    total = (halves_ref[0].astype(F32) + halves_ref[1].astype(F32)).astype(BF16)
    for k in range(out_ref.shape[0]):
        out_ref[k] = total


def shape(dims, dtype=F32):
    return jax.ShapeDtypeStruct(dims, dtype)


def to_all(block, axis):
    count = lax.axis_size(axis)
    return lax.all_to_all(jnp.broadcast_to(block[None], (count,) + block.shape), axis, 0, 0)


def flip(block, axis, bit):
    return lax.ppermute(block, axis, [(k, k ^ bit) for k in range(lax.axis_size(axis))])


def swap(block, axis):
    return flip(block, axis, 1)


def on_device(layer_input, proj_weight, ssd_input, log_decay, out_grad):
    steps, width = layer_input.shape
    heads = log_decay.shape[1]
    slabs = lax.axis_size(TM)
    groups = lax.axis_size("z")
    rows_here = proj_weight.shape[0]
    core = lax.axis_index("core").reshape(1)
    share = ssd_input.shape[1] // slabs
    logt = log_decay.T

    line_w = to_all(proj_weight, "ylo")
    own_w = to_all(line_w, "x").reshape(-1, rows_here, width)
    other_w = swap(own_w, "core")
    xet, dyft, ds = call(
        prepare,
        (
            shape(ssd_input.shape[::-1]),
            shape(ssd_input.shape[::-1]),
            shape((heads, N)),
        ),
        10**7,
        ssd_input,
        out_grad,
        log_decay,
        logt,
    )
    other_w, xet, dyft, ds = lax.optimization_barrier((other_w, xet, dyft, ds))
    partial = call(
        partial_kernel,
        shape((groups, steps + EXTRA_ROWS, 2 * N)),
        2 * steps * width * slabs * rows_here,
        core,
        layer_input,
        own_w,
        other_w,
        smem=1,
    )
    pieces = lax.all_to_all(partial.astype(F16), "z", 0, 0).astype(F32)
    half_bc = call(sum_kernel, shape((steps + EXTRA_ROWS, 2 * N)), 10**6, pieces).astype(F16)
    halves = lax.all_gather(half_bc, "yhi").astype(F32)

    parts = call(
        states_kernel,
        shape((slabs, 2 * share + EXTRA_ROWS, N)),
        12 * steps * N * ssd_input.shape[1],
        halves,
        xet,
        dyft,
        ds,
    )
    shares = lax.all_to_all(parts.astype(F16), TM, 0, 0).astype(F32)
    gx, terms, inside = call(
        local_kernel,
        (
            shape(ssd_input.shape),
            shape((steps, 2 * (ssd_input.shape[1] + N))),
            shape((heads, steps)),
        ),
        10**8,
        halves,
        ssd_input,
        out_grad,
        log_decay,
        logt,
    )
    carried = call(scan_kernel, shape(shares.shape, BF16), 10**6, shares)
    arrived = lax.all_to_all(carried, TM, 0, 0)
    own_grad = call(
        bc_grad_kernel,
        shape((2 * N, steps), BF16),
        4 * steps * N * ssd_input.shape[1],
        arrived,
        terms,
    )
    near_input, _ = lax.optimization_barrier((layer_input, carried))
    pair = jnp.concatenate([near_input, flip(near_input, "x", 1)], axis=0)
    own_grad, pair = lax.optimization_barrier((own_grad, pair))
    halves_grad = lax.all_gather(own_grad, "yhi")
    grad_x, grad_log = call(
        finish_kernel,
        (shape(ssd_input.shape), shape((heads, steps))),
        10**8,
        arrived,
        halves,
        ssd_input,
        out_grad,
        log_decay,
        logt,
        gx,
        inside,
    )
    copies = call(copies_kernel, shape((groups, 2 * N, steps), BF16), 10**6, halves_grad)
    all_grads = lax.all_to_all(copies, "z", 0, 0)
    pair, _ = lax.optimization_barrier((pair, copies))
    far_pair = flip(pair, "x", 2)
    all_grads, pair, far_pair = lax.optimization_barrier((all_grads, pair, far_pair))
    columns = groups // 2
    blocks = call(
        row_blocks_kernel, shape((4, 2 * columns, rows_here, steps), BF16), 10**6, all_grads
    )
    row_grads = lax.all_to_all(blocks, "x", 0, 0)
    grad_input = call(
        grad_input_kernel,
        shape(layer_input.shape, BF16),
        2 * steps * width * slabs * rows_here,
        core,
        all_grads,
        own_w,
        other_w,
        smem=1,
    )
    row_grads, grad_input, grad_x, grad_log = lax.optimization_barrier(
        (row_grads, grad_input, grad_x, grad_log)
    )
    keep, send = call(
        grad_weight_kernel,
        (shape((columns, rows_here, width)), shape((columns, rows_here, width), BF16)),
        2 * steps * width * slabs * rows_here,
        jnp.concatenate([core, lax.axis_index("x").reshape(1)]),
        row_grads,
        pair,
        far_pair,
        smem=1,
    )
    of_chip = call(chip_sum_kernel, shape(send.shape, BF16), 10**6, keep, swap(send, "core"))
    of_line = lax.all_to_all(of_chip, "ylo", 0, 0)
    grad_weight = call(line_sum_kernel, shape(proj_weight.shape), 10**6, of_line)
    return grad_x, grad_log.T, grad_input, grad_weight


def solution(mesh):
    fine = Mesh(mesh.devices.reshape(4, 4, 2, 8, 2), TM + HEADS)
    spec = P(TM, HEADS)
    return jax.shard_map(
        on_device,
        mesh=fine,
        in_specs=(spec,) * 5,
        out_specs=(spec,) * 4,
        check_vma=False,
    )
```

```python
import jax
import jax.numpy as jnp
from jax import lax
from jax.experimental import pallas as pl
from jax.experimental.pallas import tpu as pltpu
from jax.sharding import Mesh
from jax.sharding import PartitionSpec as P

N = 128
EXTRA_ROWS = 8
LN2 = 0.6931471805599453
F32 = jnp.float32
BF16 = jnp.bfloat16
F16 = jnp.float16
HIGHEST = lax.Precision.HIGHEST
TM = ("ylo", "x", "core")
HEADS = ("z", "yhi")


def dot(a, b, precision=None):
    return jnp.dot(a, b, preferred_element_type=F32, precision=precision)


def dot_nt(a, b, precision=None):
    return lax.dot_general(
        a, b, (((1,), (1,)), ((), ())), preferred_element_type=F32, precision=precision
    )


def dot_tn(a, b):
    return lax.dot_general(a, b, (((0,), (0,)), ((), ())), preferred_element_type=F32)


def split(a):
    high = a.astype(BF16)
    return high, (a - high.astype(F32)).astype(BF16)


def dot_split(a, b):
    a_high, a_low = split(a)
    b_high, b_low = split(b)
    return dot(a_high, b_high) + dot(a_low, b_high) + dot(a_high, b_low)


def three_terms(row):
    high = row.astype(BF16).astype(F32)
    middle = (row - high).astype(BF16).astype(F32)
    low = row - high - middle
    term = lax.broadcasted_iota(jnp.int32, (EXTRA_ROWS, N), 0)
    return jnp.where(
        term == 0, high, jnp.where(term == 1, middle, jnp.where(term == 2, low, 0.0))
    )


def exponent_of(a):
    top = jnp.max(jnp.max(jnp.abs(a), axis=1, keepdims=True), axis=0, keepdims=True)
    return jnp.ceil(jnp.log(jnp.maximum(top, 1e-30)) * (1.0 / LN2)) - 14.0


def power(exponent):
    return jnp.exp(exponent * LN2)


def iotas(n):
    return (
        lax.broadcasted_iota(jnp.int32, (n, n), 0),
        lax.broadcasted_iota(jnp.int32, (n, n), 1),
    )


def head_spread(heads, width):
    size = width // heads
    row = lax.broadcasted_iota(jnp.int32, (heads, width), 0)
    col = lax.broadcasted_iota(jnp.int32, (heads, width), 1)
    return ((col >= row * size) & (col < (row + 1) * size)).astype(F32)


def call(kernel, outs, flops, *args, smem=0):
    out_list = outs if isinstance(outs, tuple) else (outs,)
    read = sum(a.size * a.dtype.itemsize for a in args)
    wrote = sum(o.size * o.dtype.itemsize for o in out_list)
    spaces = [pltpu.SMEM if k < smem else pltpu.VMEM for k in range(len(args))]
    return pl.pallas_call(
        kernel,
        out_shape=outs,
        in_specs=[pl.BlockSpec(memory_space=space) for space in spaces],
        out_specs=jax.tree.map(lambda _: pl.BlockSpec(memory_space=pltpu.VMEM), outs),
        cost_estimate=pl.CostEstimate(
            flops=flops, bytes_accessed=read + wrote, transcendentals=0
        ),
        compiler_params=pltpu.CompilerParams(vmem_limit_bytes=16 * 2**20),
    )(*args)


def decay_sums(log_ref, logt_ref):
    row, col = iotas(log_ref.shape[0])
    cum = dot((row >= col).astype(F32), log_ref[...], HIGHEST)
    cumt = dot(logt_ref[...], (row <= col).astype(F32), HIGHEST)
    return cum, cumt


def decay_factors(cum, width):
    spread = head_spread(cum.shape[1], width)
    last = cum[cum.shape[0] - 1 :, :]
    return dot(jnp.exp(last - cum), spread, HIGHEST), dot(jnp.exp(cum), spread, HIGHEST)


def prepare(x_ref, dy_ref, log_ref, logt_ref, xet_ref, dyft_ref, ds_ref):
    steps = log_ref.shape[0]
    cum, cumt = decay_sums(log_ref, logt_ref)
    to_end, from_start = decay_factors(cum, x_ref.shape[1])
    xet_ref[...] = (x_ref[...] * to_end).T
    dyft_ref[...] = (dy_ref[...] * from_start).T
    ds_ref[...] = jnp.broadcast_to(cumt[:, steps - 1 : steps], ds_ref.shape)


def blocks_of(first, own_ref, other_ref, group, lines):
    column, half = divmod(group, 2)
    rows = []
    for line in (2 * half, 2 * half + 1):
        at = line * lines + column
        own, other = own_ref[at], other_ref[at]
        rows += [jnp.where(first, own, other), jnp.where(first, other, own)]
    return jnp.concatenate(rows, axis=0)


def partial_kernel(core_ref, x_ref, own_ref, other_ref, out_ref):
    first = core_ref[0] == 0
    x = x_ref[...]
    steps = x.shape[0]
    groups, _, columns = out_ref.shape
    top = jnp.zeros((steps, columns), F32)
    for group in range(groups):
        part = dot_nt(x, blocks_of(first, own_ref, other_ref, group, groups // 2))
        top = jnp.maximum(top, jnp.abs(part))
        out_ref[group, :steps, :] = part
    exponent = exponent_of(top)
    scale = power(-exponent)
    for group in range(groups):
        out_ref[group, :steps, :] = out_ref[group, :steps, :] * scale
        out_ref[group, steps:, :] = jnp.broadcast_to(exponent, (EXTRA_ROWS, columns))


def sum_kernel(pieces_ref, out_ref):
    pieces, rows, columns = pieces_ref.shape
    steps = rows - EXTRA_ROWS
    exponents = [pieces_ref[k, steps:, :] for k in range(pieces)]
    top = exponents[0]
    for exponent in exponents[1:]:
        top = jnp.maximum(top, exponent)
    top = top + jnp.ceil(jnp.log(1.0 * pieces) / LN2)
    total = jnp.zeros((steps, columns), F32)
    for k in range(pieces):
        total = total + pieces_ref[k, :steps, :] * power(exponents[k] - top)[:1, :]
    out_ref[:steps, :] = total
    out_ref[steps:, :] = top


def whole_bc(halves_ref):
    steps = halves_ref.shape[1] - EXTRA_ROWS
    bc = sum(
        halves_ref[k, :steps, :] * power(halves_ref[k, steps : steps + 1, :]) for k in range(2)
    )
    return bc[:, :N], bc[:, N:]


def states_kernel(halves_ref, xet_ref, dyft_ref, ds_ref, out_ref):
    b_rows, c_rows = whole_bc(halves_ref)
    heads = ds_ref.shape[0]
    parts, rows, _ = out_ref.shape
    half = (rows - EXTRA_ROWS) // 2
    state = dot_split(xet_ref[...], b_rows)
    grad = dot_split(dyft_ref[...], c_rows)
    state_exponent = exponent_of(state)
    grad_exponent = exponent_of(grad)
    out_ref[:, :half, :] = (state * power(-state_exponent)).reshape(parts, half, N)
    out_ref[:, half : 2 * half, :] = (grad * power(-grad_exponent)).reshape(parts, half, N)
    row = lax.broadcasted_iota(jnp.int32, (EXTRA_ROWS, N), 0)
    for head in range(heads):
        terms = jnp.where(row == 3, state_exponent, three_terms(ds_ref[head : head + 1, :]))
        terms = jnp.where(row == 4, grad_exponent, terms)
        for part in range(head * parts // heads, (head + 1) * parts // heads):
            out_ref[part, 2 * half :, :] = terms


def local_kernel(halves_ref, x_ref, dy_ref, log_ref, logt_ref, gx_ref, terms_ref, inside_ref):
    b_rows, c_rows = (rows.astype(BF16) for rows in whole_bc(halves_ref))
    steps, heads = log_ref.shape
    size = x_ref.shape[1] // heads
    row, col = iotas(steps)
    later = row <= col
    at_or_after = (row >= col).astype(BF16)
    bct = dot_nt(b_rows, c_rows)
    pair_sum = jnp.zeros((steps, steps), F32)
    cum, cumt = decay_sums(log_ref, logt_ref)
    for h in range(heads):
        x = x_ref[:, h * size : (h + 1) * size].astype(BF16)
        dy = dy_ref[:, h * size : (h + 1) * size].astype(BF16)
        gap = cumt[h : h + 1, :] - cum[:, h : h + 1]
        decay = jnp.where(later, jnp.exp(jnp.minimum(gap, 0.0)), 0.0)
        decayed = decay * dot_nt(x, dy)
        pair_sum = pair_sum + decayed
        gx_ref[:, h * size : (h + 1) * size] = dot((decay * bct).astype(BF16), dy)
        reach = dot((decayed * bct).astype(BF16), at_or_after)
        inside_ref[h : h + 1, :] = jnp.sum(jnp.where(row < col, reach, 0.0), axis=0, keepdims=True)
    width = x_ref.shape[1]
    to_end, from_start = decay_factors(cum, width)
    terms_ref[:, :width] = x_ref[...] * to_end
    terms_ref[:, width : 2 * width] = dy_ref[...] * from_start
    terms_ref[:, 2 * width : 2 * width + N] = dot(pair_sum.astype(BF16), c_rows)
    terms_ref[:, 2 * width + N :] = dot(pair_sum.T.astype(BF16), b_rows)


def scan_kernel(parts_ref, out_ref):
    slabs, rows, _ = out_ref.shape
    rows -= EXTRA_ROWS
    half = rows // 2

    def extra(t, k):
        return parts_ref[t, rows + k : rows + k + 1, :]

    decays = [jnp.exp(extra(t, 0) + extra(t, 1) + extra(t, 2)) for t in range(slabs)]
    grads = [jnp.zeros((half, N), F32)]
    for t in range(slabs - 1, 0, -1):
        grads.append(decays[t] * grads[-1] + power(extra(t, 4)) * parts_ref[t, half:rows, :])
    grads = grads[::-1]
    state = jnp.zeros((half, N), F32)
    for t in range(slabs):
        out_ref[t, :half, :] = state.astype(BF16)
        out_ref[t, half:rows, :] = grads[t].astype(BF16)
        product = jnp.sum(state * grads[t], axis=0, keepdims=True)
        out_ref[t, rows:, :] = three_terms(product).astype(BF16)
        state = decays[t] * state + power(extra(t, 3)) * parts_ref[t, :half, :]


def entering(in_ref):
    parts, rows, _ = in_ref.shape
    half = (rows - EXTRA_ROWS) // 2
    state = in_ref[:, :half, :].reshape(parts * half, N)
    grad = in_ref[:, half : 2 * half, :].reshape(parts * half, N)
    return state, grad


def bc_grad_kernel(in_ref, terms_ref, out_ref):
    state, grad = entering(in_ref)
    width = state.shape[0]
    from_grad = dot(terms_ref[:, :width].astype(BF16), grad)
    from_state = dot(terms_ref[:, width : 2 * width].astype(BF16), state)
    out_ref[:N, :] = (terms_ref[:, 2 * width : 2 * width + N] + from_grad).T.astype(BF16)
    out_ref[N:, :] = (terms_ref[:, 2 * width + N :] + from_state).T.astype(BF16)


def finish_kernel(in_ref, halves_ref, x_ref, dy_ref, log_ref, logt_ref, gx_ref, inside_ref, out_ref, out_log_ref):
    state, grad = entering(in_ref)
    b_rows, c_rows = (rows.astype(BF16) for rows in whole_bc(halves_ref))
    steps, heads = log_ref.shape
    width = x_ref.shape[1]
    row, col = iotas(steps)
    cum, cumt = decay_sums(log_ref, logt_ref)
    to_end, from_start = decay_factors(cum, width)
    b_state = to_end * dot_nt(b_rows, grad)
    c_state = from_start * dot_nt(c_rows, state)
    out_ref[...] = gx_ref[...] + b_state
    spread = head_spread(heads, width)
    earlier = dot_nt(spread, c_state * dy_ref[...], HIGHEST)
    later = dot_nt(spread, b_state * x_ref[...], HIGHEST)
    parts = in_ref.shape[0]
    products = jnp.sum(in_ref[:, -EXTRA_ROWS:, :].astype(F32), axis=1)
    products = jnp.sum(products.reshape(heads, parts // heads, N), axis=1)
    across = jnp.sum(products, axis=1, keepdims=True)
    across = across * jnp.exp(cumt[:, steps - 1 : steps])
    out_log_ref[...] = (
        inside_ref[...]
        + dot(earlier, (row >= col).astype(F32), HIGHEST)
        + dot(later, (row < col).astype(F32), HIGHEST)
        + across
    )


def grad_input_kernel(core_ref, grads_ref, own_ref, other_ref, out_ref):
    first = core_ref[0] == 0
    groups = grads_ref.shape[0]
    total = jnp.zeros(out_ref.shape, F32)
    for group in range(groups):
        rows = blocks_of(first, own_ref, other_ref, group, groups // 2)
        total = total + dot_tn(grads_ref[group], rows)
    out_ref[...] = total.astype(BF16)


def row_blocks_kernel(grads_ref, out_ref):
    lines, _, rows, _ = out_ref.shape
    for group in range(grads_ref.shape[0]):
        column, high = divmod(group, 2)
        for k in range(2):
            for core in range(2):
                at = (2 * k + core) * rows
                out_ref[2 * high + k, 2 * column + core] = grads_ref[group, at : at + rows, :]


def grad_weight_kernel(place_ref, grads_ref, low_ref, high_ref, keep_ref, send_ref):
    first = place_ref[0] == 0
    line = place_ref[1]
    columns, rows, width = keep_ref.shape
    x = jnp.concatenate([low_ref[...], high_ref[...]], axis=0)
    for column in range(columns):
        grads = jnp.concatenate(
            [
                grads_ref[line ^ k, 2 * column : 2 * column + 2].reshape(2 * rows, -1)
                for k in range(grads_ref.shape[0])
            ],
            axis=1,
        )
        part = dot(grads, x)
        one, other = part[:rows], part[rows:]
        keep_ref[column] = jnp.where(first, one, other)
        send_ref[column] = jnp.where(first, other, one).astype(BF16)


def chip_sum_kernel(own_ref, other_ref, out_ref):
    for k in range(out_ref.shape[0]):
        out_ref[k] = (own_ref[k] + other_ref[k].astype(F32)).astype(BF16)


def line_sum_kernel(parts_ref, out_ref):
    total = parts_ref[0].astype(F32)
    for k in range(1, parts_ref.shape[0]):
        total = total + parts_ref[k].astype(F32)
    out_ref[...] = total


def copies_kernel(halves_ref, out_ref):
    total = (halves_ref[0].astype(F32) + halves_ref[1].astype(F32)).astype(BF16)
    for k in range(out_ref.shape[0]):
        out_ref[k] = total


def shape(dims, dtype=F32):
    return jax.ShapeDtypeStruct(dims, dtype)


def to_all(block, axis):
    count = lax.axis_size(axis)
    return lax.all_to_all(jnp.broadcast_to(block[None], (count,) + block.shape), axis, 0, 0)


def flip(block, axis, bit):
    return lax.ppermute(block, axis, [(k, k ^ bit) for k in range(lax.axis_size(axis))])


def swap(block, axis):
    return flip(block, axis, 1)


def on_device(layer_input, proj_weight, ssd_input, log_decay, out_grad):
    steps, width = layer_input.shape
    heads = log_decay.shape[1]
    slabs = lax.axis_size(TM)
    groups = lax.axis_size("z")
    rows_here = proj_weight.shape[0]
    core = lax.axis_index("core").reshape(1)
    share = ssd_input.shape[1] // slabs
    logt = log_decay.T

    line_w = to_all(proj_weight, "ylo")
    own_w = to_all(line_w, "x").reshape(-1, rows_here, width)
    other_w = swap(own_w, "core")
    xet, dyft, ds = call(
        prepare,
        (
            shape(ssd_input.shape[::-1]),
            shape(ssd_input.shape[::-1]),
            shape((heads, N)),
        ),
        10**7,
        ssd_input,
        out_grad,
        log_decay,
        logt,
    )
    other_w, xet, dyft, ds = lax.optimization_barrier((other_w, xet, dyft, ds))
    partial = call(
        partial_kernel,
        shape((groups, steps + EXTRA_ROWS, 2 * N)),
        2 * steps * width * slabs * rows_here,
        core,
        layer_input,
        own_w,
        other_w,
        smem=1,
    )
    pieces = lax.all_to_all(partial.astype(F16), "z", 0, 0).astype(F32)
    half_bc = call(sum_kernel, shape((steps + EXTRA_ROWS, 2 * N)), 10**6, pieces).astype(F16)
    halves = lax.all_gather(half_bc, "yhi").astype(F32)

    parts = call(
        states_kernel,
        shape((slabs, 2 * share + EXTRA_ROWS, N)),
        12 * steps * N * ssd_input.shape[1],
        halves,
        xet,
        dyft,
        ds,
    )
    shares = lax.all_to_all(parts.astype(F16), TM, 0, 0).astype(F32)
    gx, terms, inside = call(
        local_kernel,
        (
            shape(ssd_input.shape),
            shape((steps, 2 * (ssd_input.shape[1] + N))),
            shape((heads, steps)),
        ),
        10**8,
        halves,
        ssd_input,
        out_grad,
        log_decay,
        logt,
    )
    carried = call(scan_kernel, shape(shares.shape, BF16), 10**6, shares)
    arrived = lax.all_to_all(carried, TM, 0, 0)
    own_grad = call(
        bc_grad_kernel,
        shape((2 * N, steps), BF16),
        4 * steps * N * ssd_input.shape[1],
        arrived,
        terms,
    )
    near_input, _ = lax.optimization_barrier((layer_input, carried))
    pair = jnp.concatenate([near_input, flip(near_input, "x", 1)], axis=0)
    own_grad, pair = lax.optimization_barrier((own_grad, pair))
    halves_grad = lax.all_gather(own_grad, "yhi")
    grad_x, grad_log = call(
        finish_kernel,
        (shape(ssd_input.shape), shape((heads, steps))),
        10**8,
        arrived,
        halves,
        ssd_input,
        out_grad,
        log_decay,
        logt,
        gx,
        inside,
    )
    copies = call(copies_kernel, shape((groups, 2 * N, steps), BF16), 10**6, halves_grad)
    all_grads = lax.all_to_all(copies, "z", 0, 0)
    pair, _ = lax.optimization_barrier((pair, copies))
    far_pair = flip(pair, "x", 2)
    all_grads, pair, far_pair, grad_x, grad_log = lax.optimization_barrier(
        (all_grads, pair, far_pair, grad_x, grad_log)
    )
    columns = groups // 2
    blocks = call(
        row_blocks_kernel, shape((4, 2 * columns, rows_here, steps), BF16), 10**6, all_grads
    )
    row_grads = lax.all_to_all(blocks, "x", 0, 0)
    keep, send = call(
        grad_weight_kernel,
        (shape((columns, rows_here, width)), shape((columns, rows_here, width), BF16)),
        2 * steps * width * slabs * rows_here,
        jnp.concatenate([core, lax.axis_index("x").reshape(1)]),
        row_grads,
        pair,
        far_pair,
        smem=1,
    )
    from_core = swap(send, "core")
    all_grads, _ = lax.optimization_barrier((all_grads, send))
    grad_input = call(
        grad_input_kernel,
        shape(layer_input.shape, BF16),
        2 * steps * width * slabs * rows_here,
        core,
        all_grads,
        own_w,
        other_w,
        smem=1,
    )
    from_core, grad_input = lax.optimization_barrier((from_core, grad_input))
    of_chip = call(chip_sum_kernel, shape(send.shape, BF16), 10**6, keep, from_core)
    of_line = lax.all_to_all(of_chip, "ylo", 0, 0)
    grad_weight = call(line_sum_kernel, shape(proj_weight.shape), 10**6, of_line)
    return grad_x, grad_log.T, grad_input, grad_weight


def solution(mesh):
    fine = Mesh(mesh.devices.reshape(4, 4, 2, 8, 2), TM + HEADS)
    spec = P(TM, HEADS)
    return jax.shard_map(
        on_device,
        mesh=fine,
        in_specs=(spec,) * 5,
        out_specs=(spec,) * 4,
        check_vma=False,
    )
```

```python
import jax
import jax.numpy as jnp
from jax import lax
from jax.experimental import pallas as pl
from jax.experimental.pallas import tpu as pltpu
from jax.sharding import Mesh
from jax.sharding import PartitionSpec as P

N = 128
EXTRA_ROWS = 8
LN2 = 0.6931471805599453
SCALE = 256.0
F32 = jnp.float32
BF16 = jnp.bfloat16
F16 = jnp.float16
HIGHEST = lax.Precision.HIGHEST
TM = ("ylo", "x", "core")
HEADS = ("z", "yhi")


def dot(a, b, precision=None):
    return jnp.dot(a, b, preferred_element_type=F32, precision=precision)


def dot_nt(a, b, precision=None):
    return lax.dot_general(
        a, b, (((1,), (1,)), ((), ())), preferred_element_type=F32, precision=precision
    )


def dot_tn(a, b):
    return lax.dot_general(a, b, (((0,), (0,)), ((), ())), preferred_element_type=F32)


def split(a):
    high = a.astype(BF16)
    return high, (a - high.astype(F32)).astype(BF16)


def dot_split(a, b):
    a_high, a_low = split(a)
    b_high, b_low = split(b)
    return dot(a_high, b_high) + dot(a_low, b_high) + dot(a_high, b_low)


def three_terms(row):
    high = row.astype(BF16).astype(F32)
    middle = (row - high).astype(BF16).astype(F32)
    low = row - high - middle
    term = lax.broadcasted_iota(jnp.int32, (EXTRA_ROWS, N), 0)
    return jnp.where(
        term == 0, high, jnp.where(term == 1, middle, jnp.where(term == 2, low, 0.0))
    )


def exponent_of(a):
    top = jnp.max(jnp.max(jnp.abs(a), axis=1, keepdims=True), axis=0, keepdims=True)
    return jnp.ceil(jnp.log(jnp.maximum(top, 1e-30)) * (1.0 / LN2)) - 14.0


def power(exponent):
    return jnp.exp(exponent * LN2)


def iotas(n):
    return (
        lax.broadcasted_iota(jnp.int32, (n, n), 0),
        lax.broadcasted_iota(jnp.int32, (n, n), 1),
    )


def head_spread(heads, width):
    size = width // heads
    row = lax.broadcasted_iota(jnp.int32, (heads, width), 0)
    col = lax.broadcasted_iota(jnp.int32, (heads, width), 1)
    return ((col >= row * size) & (col < (row + 1) * size)).astype(F32)


def call(kernel, outs, flops, *args, smem=0):
    out_list = outs if isinstance(outs, tuple) else (outs,)
    read = sum(a.size * a.dtype.itemsize for a in args)
    wrote = sum(o.size * o.dtype.itemsize for o in out_list)
    spaces = [pltpu.SMEM if k < smem else pltpu.VMEM for k in range(len(args))]
    return pl.pallas_call(
        kernel,
        out_shape=outs,
        in_specs=[pl.BlockSpec(memory_space=space) for space in spaces],
        out_specs=jax.tree.map(lambda _: pl.BlockSpec(memory_space=pltpu.VMEM), outs),
        cost_estimate=pl.CostEstimate(
            flops=flops, bytes_accessed=read + wrote, transcendentals=0
        ),
        compiler_params=pltpu.CompilerParams(vmem_limit_bytes=16 * 2**20),
    )(*args)


def decay_sums(log_ref, logt_ref):
    row, col = iotas(log_ref.shape[0])
    cum = dot((row >= col).astype(F32), log_ref[...], HIGHEST)
    cumt = dot(logt_ref[...], (row <= col).astype(F32), HIGHEST)
    return cum, cumt


def decay_factors(cum, width):
    spread = head_spread(cum.shape[1], width)
    last = cum[cum.shape[0] - 1 :, :]
    return dot(jnp.exp(last - cum), spread, HIGHEST), dot(jnp.exp(cum), spread, HIGHEST)


def prepare(x_ref, dy_ref, log_ref, logt_ref, xet_ref, dyft_ref, ds_ref):
    steps = log_ref.shape[0]
    cum, cumt = decay_sums(log_ref, logt_ref)
    to_end, from_start = decay_factors(cum, x_ref.shape[1])
    xet_ref[...] = (x_ref[...] * to_end).T
    dyft_ref[...] = (dy_ref[...] * from_start).T
    ds_ref[...] = jnp.broadcast_to(cumt[:, steps - 1 : steps], ds_ref.shape)


def blocks_of(first, own_ref, other_ref, group, lines):
    column, half = divmod(group, 2)
    rows = []
    for line in (2 * half, 2 * half + 1):
        at = line * lines + column
        own, other = own_ref[at], other_ref[at]
        rows += [jnp.where(first, own, other), jnp.where(first, other, own)]
    return jnp.concatenate(rows, axis=0)


def partial_kernel(core_ref, x_ref, own_ref, other_ref, out_ref):
    first = core_ref[0] == 0
    x = x_ref[...]
    steps = x.shape[0]
    groups, _, columns = out_ref.shape
    top = jnp.zeros((steps, columns), F32)
    for group in range(groups):
        part = dot_nt(x, blocks_of(first, own_ref, other_ref, group, groups // 2))
        top = jnp.maximum(top, jnp.abs(part))
        out_ref[group, :steps, :] = part
    exponent = exponent_of(top)
    scale = power(-exponent)
    for group in range(groups):
        out_ref[group, :steps, :] = out_ref[group, :steps, :] * scale
        out_ref[group, steps:, :] = jnp.broadcast_to(exponent, (EXTRA_ROWS, columns))


def sum_kernel(pieces_ref, out_ref):
    pieces, rows, columns = pieces_ref.shape
    steps = rows - EXTRA_ROWS
    exponents = [pieces_ref[k, steps:, :] for k in range(pieces)]
    top = exponents[0]
    for exponent in exponents[1:]:
        top = jnp.maximum(top, exponent)
    top = top + jnp.ceil(jnp.log(1.0 * pieces) / LN2)
    total = jnp.zeros((steps, columns), F32)
    for k in range(pieces):
        total = total + pieces_ref[k, :steps, :] * power(exponents[k] - top)[:1, :]
    out_ref[:steps, :] = total
    out_ref[steps:, :] = top


def whole_bc(halves_ref):
    steps = halves_ref.shape[1] - EXTRA_ROWS
    bc = sum(
        halves_ref[k, :steps, :] * power(halves_ref[k, steps : steps + 1, :]) for k in range(2)
    )
    return bc[:, :N], bc[:, N:]


def states_kernel(halves_ref, xet_ref, dyft_ref, ds_ref, out_ref):
    b_rows, c_rows = whole_bc(halves_ref)
    heads = ds_ref.shape[0]
    parts, rows, _ = out_ref.shape
    half = (rows - EXTRA_ROWS) // 2
    state = dot_split(xet_ref[...], b_rows)
    grad = dot_split(dyft_ref[...], c_rows)
    state_exponent = exponent_of(state)
    grad_exponent = exponent_of(grad)
    out_ref[:, :half, :] = (state * power(-state_exponent)).reshape(parts, half, N)
    out_ref[:, half : 2 * half, :] = (grad * power(-grad_exponent)).reshape(parts, half, N)
    row = lax.broadcasted_iota(jnp.int32, (EXTRA_ROWS, N), 0)
    for head in range(heads):
        terms = jnp.where(row == 3, state_exponent, three_terms(SCALE * ds_ref[head : head + 1, :]))
        terms = jnp.where(row == 4, grad_exponent, terms)
        for part in range(head * parts // heads, (head + 1) * parts // heads):
            out_ref[part, 2 * half :, :] = terms


def local_kernel(halves_ref, x_ref, dy_ref, log_ref, logt_ref, gx_ref, terms_ref, inside_ref):
    b_rows, c_rows = (rows.astype(BF16) for rows in whole_bc(halves_ref))
    steps, heads = log_ref.shape
    size = x_ref.shape[1] // heads
    row, col = iotas(steps)
    later = row <= col
    at_or_after = (row >= col).astype(BF16)
    bct = dot_nt(b_rows, c_rows)
    pair_sum = jnp.zeros((steps, steps), F32)
    cum, cumt = decay_sums(log_ref, logt_ref)
    for h in range(heads):
        x = x_ref[:, h * size : (h + 1) * size].astype(BF16)
        dy = dy_ref[:, h * size : (h + 1) * size].astype(BF16)
        gap = cumt[h : h + 1, :] - cum[:, h : h + 1]
        decay = jnp.where(later, jnp.exp(jnp.minimum(gap, 0.0)), 0.0)
        decayed = decay * dot_nt(x, dy)
        pair_sum = pair_sum + decayed
        gx_ref[:, h * size : (h + 1) * size] = dot((decay * bct).astype(BF16), dy)
        reach = dot((decayed * bct).astype(BF16), at_or_after)
        inside_ref[h : h + 1, :] = jnp.sum(jnp.where(row < col, reach, 0.0), axis=0, keepdims=True)
    width = x_ref.shape[1]
    to_end, from_start = decay_factors(cum, width)
    terms_ref[:, :width] = x_ref[...] * to_end
    terms_ref[:, width : 2 * width] = dy_ref[...] * from_start
    terms_ref[:, 2 * width : 2 * width + N] = dot(pair_sum.astype(BF16), c_rows)
    terms_ref[:, 2 * width + N :] = dot(pair_sum.T.astype(BF16), b_rows)


def scan_kernel(parts_ref, out_ref):
    slabs, rows, _ = out_ref.shape
    rows -= EXTRA_ROWS
    half = rows // 2

    def extra(t, k):
        return parts_ref[t, rows + k : rows + k + 1, :]

    decays = [jnp.exp((extra(t, 0) + extra(t, 1) + extra(t, 2)) / SCALE) for t in range(slabs)]
    grads = [jnp.zeros((half, N), F32)]
    for t in range(slabs - 1, 0, -1):
        grads.append(decays[t] * grads[-1] + power(extra(t, 4)) * parts_ref[t, half:rows, :])
    grads = grads[::-1]
    state = jnp.zeros((half, N), F32)
    for t in range(slabs):
        out_ref[t, :half, :] = state.astype(BF16)
        out_ref[t, half:rows, :] = grads[t].astype(BF16)
        product = jnp.sum(state * grads[t], axis=0, keepdims=True)
        out_ref[t, rows:, :] = three_terms(product).astype(BF16)
        state = decays[t] * state + power(extra(t, 3)) * parts_ref[t, :half, :]


def entering(in_ref):
    parts, rows, _ = in_ref.shape
    half = (rows - EXTRA_ROWS) // 2
    state = in_ref[:, :half, :].reshape(parts * half, N)
    grad = in_ref[:, half : 2 * half, :].reshape(parts * half, N)
    return state, grad


def bc_grad_kernel(in_ref, terms_ref, out_ref):
    state, grad = entering(in_ref)
    width = state.shape[0]
    from_grad = dot(terms_ref[:, :width].astype(BF16), grad)
    from_state = dot(terms_ref[:, width : 2 * width].astype(BF16), state)
    out_ref[:N, :] = (terms_ref[:, 2 * width : 2 * width + N] + from_grad).T.astype(BF16)
    out_ref[N:, :] = (terms_ref[:, 2 * width + N :] + from_state).T.astype(BF16)


def finish_kernel(in_ref, halves_ref, x_ref, dy_ref, log_ref, logt_ref, gx_ref, inside_ref, out_ref, out_log_ref):
    state, grad = entering(in_ref)
    b_rows, c_rows = (rows.astype(BF16) for rows in whole_bc(halves_ref))
    steps, heads = log_ref.shape
    width = x_ref.shape[1]
    row, col = iotas(steps)
    cum, cumt = decay_sums(log_ref, logt_ref)
    to_end, from_start = decay_factors(cum, width)
    b_state = to_end * dot_nt(b_rows, grad)
    c_state = from_start * dot_nt(c_rows, state)
    out_ref[...] = gx_ref[...] + b_state
    spread = head_spread(heads, width)
    earlier = dot_nt(spread, c_state * dy_ref[...], HIGHEST)
    later = dot_nt(spread, b_state * x_ref[...], HIGHEST)
    parts = in_ref.shape[0]
    products = jnp.sum(in_ref[:, -EXTRA_ROWS:, :].astype(F32), axis=1)
    products = jnp.sum(products.reshape(heads, parts // heads, N), axis=1)
    across = jnp.sum(products, axis=1, keepdims=True)
    across = across * jnp.exp(cumt[:, steps - 1 : steps])
    out_log_ref[...] = (
        inside_ref[...]
        + dot(earlier, (row >= col).astype(F32), HIGHEST)
        + dot(later, (row < col).astype(F32), HIGHEST)
        + across
    )


def grad_input_kernel(core_ref, grads_ref, own_ref, other_ref, out_ref):
    first = core_ref[0] == 0
    groups = grads_ref.shape[0]
    total = jnp.zeros(out_ref.shape, F32)
    for group in range(groups):
        rows = blocks_of(first, own_ref, other_ref, group, groups // 2)
        total = total + dot_tn(grads_ref[group], rows)
    out_ref[...] = total.astype(BF16)


def row_blocks_kernel(grads_ref, out_ref):
    lines, _, rows, _ = out_ref.shape
    for group in range(grads_ref.shape[0]):
        column, high = divmod(group, 2)
        for k in range(2):
            for core in range(2):
                at = (2 * k + core) * rows
                out_ref[2 * high + k, 2 * column + core] = grads_ref[group, at : at + rows, :]


def grad_weight_kernel(place_ref, grads_ref, low_ref, high_ref, keep_ref, send_ref):
    first = place_ref[0] == 0
    line = place_ref[1]
    columns, rows, width = keep_ref.shape
    x = jnp.concatenate([low_ref[...], high_ref[...]], axis=0)
    for column in range(columns):
        grads = jnp.concatenate(
            [
                grads_ref[line ^ k, 2 * column : 2 * column + 2].reshape(2 * rows, -1)
                for k in range(grads_ref.shape[0])
            ],
            axis=1,
        )
        part = dot(grads, x)
        one, other = part[:rows], part[rows:]
        keep_ref[column] = jnp.where(first, one, other)
        send_ref[column] = jnp.where(first, other, one).astype(BF16)


def chip_sum_kernel(own_ref, other_ref, out_ref):
    for k in range(out_ref.shape[0]):
        out_ref[k] = (own_ref[k] + other_ref[k].astype(F32)).astype(BF16)


def line_sum_kernel(parts_ref, out_ref):
    total = parts_ref[0].astype(F32)
    for k in range(1, parts_ref.shape[0]):
        total = total + parts_ref[k].astype(F32)
    out_ref[...] = total


def copies_kernel(halves_ref, out_ref):
    total = (halves_ref[0].astype(F32) + halves_ref[1].astype(F32)).astype(BF16)
    for k in range(out_ref.shape[0]):
        out_ref[k] = total


def shape(dims, dtype=F32):
    return jax.ShapeDtypeStruct(dims, dtype)


def to_all(block, axis):
    count = lax.axis_size(axis)
    return lax.all_to_all(jnp.broadcast_to(block[None], (count,) + block.shape), axis, 0, 0)


def flip(block, axis, bit):
    return lax.ppermute(block, axis, [(k, k ^ bit) for k in range(lax.axis_size(axis))])


def swap(block, axis):
    return flip(block, axis, 1)


def on_device(layer_input, proj_weight, ssd_input, log_decay, out_grad):
    steps, width = layer_input.shape
    heads = log_decay.shape[1]
    slabs = lax.axis_size(TM)
    groups = lax.axis_size("z")
    rows_here = proj_weight.shape[0]
    core = lax.axis_index("core").reshape(1)
    share = ssd_input.shape[1] // slabs
    logt = log_decay.T

    line_w = to_all(proj_weight, "ylo")
    own_w = to_all(line_w, "x").reshape(-1, rows_here, width)
    other_w = swap(own_w, "core")
    xet, dyft, ds = call(
        prepare,
        (
            shape(ssd_input.shape[::-1]),
            shape(ssd_input.shape[::-1]),
            shape((heads, N)),
        ),
        10**7,
        ssd_input,
        out_grad,
        log_decay,
        logt,
    )
    other_w, xet, dyft, ds = lax.optimization_barrier((other_w, xet, dyft, ds))
    partial = call(
        partial_kernel,
        shape((groups, steps + EXTRA_ROWS, 2 * N)),
        2 * steps * width * slabs * rows_here,
        core,
        layer_input,
        own_w,
        other_w,
        smem=1,
    )
    pieces = lax.all_to_all(partial.astype(F16), "z", 0, 0).astype(F32)
    half_bc = call(sum_kernel, shape((steps + EXTRA_ROWS, 2 * N)), 10**6, pieces).astype(F16)
    halves = lax.all_gather(half_bc, "yhi").astype(F32)

    parts = call(
        states_kernel,
        shape((slabs, 2 * share + EXTRA_ROWS, N)),
        12 * steps * N * ssd_input.shape[1],
        halves,
        xet,
        dyft,
        ds,
    )
    shares = lax.all_to_all(parts.astype(F16), TM, 0, 0).astype(F32)
    gx, terms, inside = call(
        local_kernel,
        (
            shape(ssd_input.shape),
            shape((steps, 2 * (ssd_input.shape[1] + N))),
            shape((heads, steps)),
        ),
        10**8,
        halves,
        ssd_input,
        out_grad,
        log_decay,
        logt,
    )
    carried = call(scan_kernel, shape(shares.shape, BF16), 10**6, shares)
    arrived = lax.all_to_all(carried, TM, 0, 0)
    own_grad = call(
        bc_grad_kernel,
        shape((2 * N, steps), BF16),
        4 * steps * N * ssd_input.shape[1],
        arrived,
        terms,
    )
    near_input, _ = lax.optimization_barrier((layer_input, carried))
    pair = jnp.concatenate([near_input, flip(near_input, "x", 1)], axis=0)
    own_grad, pair = lax.optimization_barrier((own_grad, pair))
    halves_grad = lax.all_gather(own_grad, "yhi")
    grad_x, grad_log = call(
        finish_kernel,
        (shape(ssd_input.shape), shape((heads, steps))),
        10**8,
        arrived,
        halves,
        ssd_input,
        out_grad,
        log_decay,
        logt,
        gx,
        inside,
    )
    copies = call(copies_kernel, shape((groups, 2 * N, steps), BF16), 10**6, halves_grad)
    all_grads = lax.all_to_all(copies, "z", 0, 0)
    pair, _ = lax.optimization_barrier((pair, copies))
    far_pair = flip(pair, "x", 2)
    all_grads, pair, far_pair, grad_x, grad_log = lax.optimization_barrier(
        (all_grads, pair, far_pair, grad_x, grad_log)
    )
    columns = groups // 2
    blocks = call(
        row_blocks_kernel, shape((4, 2 * columns, rows_here, steps), BF16), 10**6, all_grads
    )
    row_grads = lax.all_to_all(blocks, "x", 0, 0)
    keep, send = call(
        grad_weight_kernel,
        (shape((columns, rows_here, width)), shape((columns, rows_here, width), BF16)),
        2 * steps * width * slabs * rows_here,
        jnp.concatenate([core, lax.axis_index("x").reshape(1)]),
        row_grads,
        pair,
        far_pair,
        smem=1,
    )
    from_core = swap(send, "core")
    all_grads, _ = lax.optimization_barrier((all_grads, send))
    grad_input = call(
        grad_input_kernel,
        shape(layer_input.shape, BF16),
        2 * steps * width * slabs * rows_here,
        core,
        all_grads,
        own_w,
        other_w,
        smem=1,
    )
    from_core, grad_input = lax.optimization_barrier((from_core, grad_input))
    of_chip = call(chip_sum_kernel, shape(send.shape, BF16), 10**6, keep, from_core)
    of_line = lax.all_to_all(of_chip, "ylo", 0, 0)
    grad_weight = call(line_sum_kernel, shape(proj_weight.shape), 10**6, of_line)
    return grad_x, grad_log.T, grad_input, grad_weight


def solution(mesh):
    fine = Mesh(mesh.devices.reshape(4, 4, 2, 8, 2), TM + HEADS)
    spec = P(TM, HEADS)
    return jax.shard_map(
        on_device,
        mesh=fine,
        in_specs=(spec,) * 5,
        out_specs=(spec,) * 4,
        check_vma=False,
    )
```

```python
import jax
import jax.numpy as jnp
from jax import lax
from jax.experimental import pallas as pl
from jax.experimental.pallas import tpu as pltpu
from jax.sharding import Mesh
from jax.sharding import PartitionSpec as P

N = 128
EXTRA_ROWS = 8
LN2 = 0.6931471805599453
SCALE = 256.0
F32 = jnp.float32
BF16 = jnp.bfloat16
F16 = jnp.float16
HIGHEST = lax.Precision.HIGHEST
TM = ("ylo", "x", "core")
HEADS = ("z", "yhi")


def dot(a, b, precision=None):
    return jnp.dot(a, b, preferred_element_type=F32, precision=precision)


def dot_nt(a, b, precision=None):
    return lax.dot_general(
        a, b, (((1,), (1,)), ((), ())), preferred_element_type=F32, precision=precision
    )


def dot_tn(a, b):
    return lax.dot_general(a, b, (((0,), (0,)), ((), ())), preferred_element_type=F32)


def split(a):
    high = a.astype(BF16)
    return high, (a - high.astype(F32)).astype(BF16)


def dot_split(a, b):
    a_high, a_low = split(a)
    b_high, b_low = split(b)
    return dot(a_high, b_high) + dot(a_low, b_high) + dot(a_high, b_low)


def three_terms(row):
    high = row.astype(BF16).astype(F32)
    middle = (row - high).astype(BF16).astype(F32)
    low = row - high - middle
    term = lax.broadcasted_iota(jnp.int32, (EXTRA_ROWS, N), 0)
    return jnp.where(
        term == 0, high, jnp.where(term == 1, middle, jnp.where(term == 2, low, 0.0))
    )


def exponent_of(a):
    top = jnp.max(jnp.max(jnp.abs(a), axis=1, keepdims=True), axis=0, keepdims=True)
    return jnp.ceil(jnp.log(jnp.maximum(top, 1e-30)) * (1.0 / LN2)) - 14.0


def power(exponent):
    return jnp.exp(exponent * LN2)


def iotas(n):
    return (
        lax.broadcasted_iota(jnp.int32, (n, n), 0),
        lax.broadcasted_iota(jnp.int32, (n, n), 1),
    )


def head_spread(heads, width):
    size = width // heads
    row = lax.broadcasted_iota(jnp.int32, (heads, width), 0)
    col = lax.broadcasted_iota(jnp.int32, (heads, width), 1)
    return ((col >= row * size) & (col < (row + 1) * size)).astype(F32)


def call(kernel, outs, flops, *args, smem=0):
    out_list = outs if isinstance(outs, tuple) else (outs,)
    read = sum(a.size * a.dtype.itemsize for a in args)
    wrote = sum(o.size * o.dtype.itemsize for o in out_list)
    spaces = [pltpu.SMEM if k < smem else pltpu.VMEM for k in range(len(args))]
    return pl.pallas_call(
        kernel,
        out_shape=outs,
        in_specs=[pl.BlockSpec(memory_space=space) for space in spaces],
        out_specs=jax.tree.map(lambda _: pl.BlockSpec(memory_space=pltpu.VMEM), outs),
        cost_estimate=pl.CostEstimate(
            flops=flops, bytes_accessed=read + wrote, transcendentals=0
        ),
        compiler_params=pltpu.CompilerParams(vmem_limit_bytes=16 * 2**20),
    )(*args)


def decay_sums(log_ref, logt_ref):
    row, col = iotas(log_ref.shape[0])
    cum = dot((row >= col).astype(F32), log_ref[...], HIGHEST)
    cumt = dot(logt_ref[...], (row <= col).astype(F32), HIGHEST)
    return cum, cumt


def decay_factors(cum, width):
    spread = head_spread(cum.shape[1], width)
    last = cum[cum.shape[0] - 1 :, :]
    return dot(jnp.exp(last - cum), spread, HIGHEST), dot(jnp.exp(cum), spread, HIGHEST)


def prepare(x_ref, dy_ref, log_ref, logt_ref, xet_ref, dyft_ref, ds_ref):
    steps = log_ref.shape[0]
    cum, cumt = decay_sums(log_ref, logt_ref)
    to_end, from_start = decay_factors(cum, x_ref.shape[1])
    xet_ref[...] = (x_ref[...] * to_end).T
    dyft_ref[...] = (dy_ref[...] * from_start).T
    ds_ref[...] = jnp.broadcast_to(cumt[:, steps - 1 : steps], ds_ref.shape)


def blocks_of(first, own_ref, other_ref, group, lines):
    column, half = divmod(group, 2)
    rows = []
    for line in (2 * half, 2 * half + 1):
        at = line * lines + column
        own, other = own_ref[at], other_ref[at]
        rows += [jnp.where(first, own, other), jnp.where(first, other, own)]
    return jnp.concatenate(rows, axis=0)


def partial_kernel(core_ref, x_ref, own_ref, other_ref, out_ref):
    first = core_ref[0] == 0
    x = x_ref[...]
    steps = x.shape[0]
    groups, _, columns = out_ref.shape
    for group in range(groups):
        part = dot_nt(x, blocks_of(first, own_ref, other_ref, group, groups // 2))
        exponent = exponent_of(part)
        out_ref[group, :steps, :] = part * power(-exponent)
        out_ref[group, steps:, :] = jnp.broadcast_to(exponent, (EXTRA_ROWS, columns))


def sum_kernel(pieces_ref, out_ref):
    pieces, rows, columns = pieces_ref.shape
    steps = rows - EXTRA_ROWS
    exponents = [pieces_ref[k, steps:, :] for k in range(pieces)]
    top = exponents[0]
    for exponent in exponents[1:]:
        top = jnp.maximum(top, exponent)
    top = top + jnp.ceil(jnp.log(1.0 * pieces) / LN2)
    total = jnp.zeros((steps, columns), F32)
    for k in range(pieces):
        total = total + pieces_ref[k, :steps, :] * power(exponents[k] - top)[:1, :]
    out_ref[:steps, :] = total
    out_ref[steps:, :] = top


def whole_bc(halves_ref):
    steps = halves_ref.shape[1] - EXTRA_ROWS
    bc = sum(
        halves_ref[k, :steps, :] * power(halves_ref[k, steps : steps + 1, :]) for k in range(2)
    )
    return bc[:, :N], bc[:, N:]


def states_kernel(halves_ref, xet_ref, dyft_ref, ds_ref, out_ref):
    b_rows, c_rows = whole_bc(halves_ref)
    heads = ds_ref.shape[0]
    parts, rows, _ = out_ref.shape
    half = (rows - EXTRA_ROWS) // 2
    state = dot_split(xet_ref[...], b_rows)
    grad = dot_split(dyft_ref[...], c_rows)
    state_exponent = exponent_of(state)
    grad_exponent = exponent_of(grad)
    out_ref[:, :half, :] = (state * power(-state_exponent)).reshape(parts, half, N)
    out_ref[:, half : 2 * half, :] = (grad * power(-grad_exponent)).reshape(parts, half, N)
    row = lax.broadcasted_iota(jnp.int32, (EXTRA_ROWS, N), 0)
    for head in range(heads):
        terms = jnp.where(row == 3, state_exponent, three_terms(SCALE * ds_ref[head : head + 1, :]))
        terms = jnp.where(row == 4, grad_exponent, terms)
        for part in range(head * parts // heads, (head + 1) * parts // heads):
            out_ref[part, 2 * half :, :] = terms


def local_kernel(halves_ref, x_ref, dy_ref, log_ref, logt_ref, gx_ref, terms_ref, inside_ref):
    b_rows, c_rows = (rows.astype(BF16) for rows in whole_bc(halves_ref))
    steps, heads = log_ref.shape
    size = x_ref.shape[1] // heads
    row, col = iotas(steps)
    later = row <= col
    at_or_after = (row >= col).astype(BF16)
    bct = dot_nt(b_rows, c_rows)
    pair_sum = jnp.zeros((steps, steps), F32)
    cum, cumt = decay_sums(log_ref, logt_ref)
    for h in range(heads):
        x = x_ref[:, h * size : (h + 1) * size].astype(BF16)
        dy = dy_ref[:, h * size : (h + 1) * size].astype(BF16)
        gap = cumt[h : h + 1, :] - cum[:, h : h + 1]
        decay = jnp.where(later, jnp.exp(jnp.minimum(gap, 0.0)), 0.0)
        decayed = decay * dot_nt(x, dy)
        pair_sum = pair_sum + decayed
        gx_ref[:, h * size : (h + 1) * size] = dot((decay * bct).astype(BF16), dy)
        reach = dot((decayed * bct).astype(BF16), at_or_after)
        inside_ref[h : h + 1, :] = jnp.sum(jnp.where(row < col, reach, 0.0), axis=0, keepdims=True)
    width = x_ref.shape[1]
    to_end, from_start = decay_factors(cum, width)
    terms_ref[:, :width] = (x_ref[...] * to_end).astype(BF16)
    terms_ref[:, width : 2 * width] = (dy_ref[...] * from_start).astype(BF16)
    terms_ref[:, 2 * width : 2 * width + N] = dot(pair_sum.astype(BF16), c_rows).astype(BF16)
    terms_ref[:, 2 * width + N :] = dot(pair_sum.T.astype(BF16), b_rows).astype(BF16)


def scan_kernel(parts_ref, out_ref):
    slabs, rows, _ = out_ref.shape
    rows -= EXTRA_ROWS
    half = rows // 2

    def extra(t, k):
        return parts_ref[t, rows + k : rows + k + 1, :]

    decays = [jnp.exp((extra(t, 0) + extra(t, 1) + extra(t, 2)) / SCALE) for t in range(slabs)]
    grads = [jnp.zeros((half, N), F32)]
    for t in range(slabs - 1, 0, -1):
        grads.append(decays[t] * grads[-1] + power(extra(t, 4)) * parts_ref[t, half:rows, :])
    grads = grads[::-1]
    state = jnp.zeros((half, N), F32)
    for t in range(slabs):
        out_ref[t, :half, :] = state.astype(BF16)
        out_ref[t, half:rows, :] = grads[t].astype(BF16)
        product = jnp.sum(state * grads[t], axis=0, keepdims=True)
        out_ref[t, rows:, :] = three_terms(product).astype(BF16)
        state = decays[t] * state + power(extra(t, 3)) * parts_ref[t, :half, :]


def entering(in_ref):
    parts, rows, _ = in_ref.shape
    half = (rows - EXTRA_ROWS) // 2
    state = in_ref[:, :half, :].reshape(parts * half, N)
    grad = in_ref[:, half : 2 * half, :].reshape(parts * half, N)
    return state, grad


def bc_grad_kernel(in_ref, terms_ref, out_ref):
    state, grad = entering(in_ref)
    width = state.shape[0]
    from_grad = dot(terms_ref[:, :width], grad)
    from_state = dot(terms_ref[:, width : 2 * width], state)
    out_ref[:N, :] = (terms_ref[:, 2 * width : 2 * width + N].astype(F32) + from_grad).T.astype(BF16)
    out_ref[N:, :] = (terms_ref[:, 2 * width + N :].astype(F32) + from_state).T.astype(BF16)


def finish_kernel(in_ref, halves_ref, x_ref, dy_ref, log_ref, logt_ref, gx_ref, inside_ref, out_ref, out_log_ref):
    state, grad = entering(in_ref)
    b_rows, c_rows = (rows.astype(BF16) for rows in whole_bc(halves_ref))
    steps, heads = log_ref.shape
    width = x_ref.shape[1]
    row, col = iotas(steps)
    cum, cumt = decay_sums(log_ref, logt_ref)
    to_end, from_start = decay_factors(cum, width)
    b_state = to_end * dot_nt(b_rows, grad)
    c_state = from_start * dot_nt(c_rows, state)
    out_ref[...] = gx_ref[...] + b_state
    spread = head_spread(heads, width)
    earlier = dot_nt(spread, c_state * dy_ref[...], HIGHEST)
    later = dot_nt(spread, b_state * x_ref[...], HIGHEST)
    parts = in_ref.shape[0]
    products = jnp.sum(in_ref[:, -EXTRA_ROWS:, :].astype(F32), axis=1)
    products = jnp.sum(products.reshape(heads, parts // heads, N), axis=1)
    across = jnp.sum(products, axis=1, keepdims=True)
    across = across * jnp.exp(cumt[:, steps - 1 : steps])
    out_log_ref[...] = (
        inside_ref[...]
        + dot(earlier, (row >= col).astype(F32), HIGHEST)
        + dot(later, (row < col).astype(F32), HIGHEST)
        + across
    )


def grad_input_kernel(core_ref, grads_ref, own_ref, other_ref, out_ref):
    first = core_ref[0] == 0
    groups = grads_ref.shape[0]
    total = jnp.zeros(out_ref.shape, F32)
    for group in range(groups):
        rows = blocks_of(first, own_ref, other_ref, group, groups // 2)
        total = total + dot_tn(grads_ref[group], rows)
    out_ref[...] = total.astype(BF16)


def row_blocks_kernel(grads_ref, out_ref):
    lines, _, rows, _ = out_ref.shape
    for group in range(grads_ref.shape[0]):
        column, high = divmod(group, 2)
        for k in range(2):
            for core in range(2):
                at = (2 * k + core) * rows
                out_ref[2 * high + k, 2 * column + core] = grads_ref[group, at : at + rows, :]


def grad_weight_kernel(place_ref, grads_ref, low_ref, high_ref, keep_ref, send_ref):
    first = place_ref[0] == 0
    line = place_ref[1]
    columns, rows, width = keep_ref.shape
    x = jnp.concatenate([low_ref[...], high_ref[...]], axis=0)
    for column in range(columns):
        grads = jnp.concatenate(
            [
                grads_ref[line ^ k, 2 * column : 2 * column + 2].reshape(2 * rows, -1)
                for k in range(grads_ref.shape[0])
            ],
            axis=1,
        )
        part = dot(grads, x)
        one, other = part[:rows], part[rows:]
        keep_ref[column] = jnp.where(first, one, other)
        send_ref[column] = jnp.where(first, other, one).astype(BF16)


def chip_sum_kernel(own_ref, other_ref, out_ref):
    for k in range(out_ref.shape[0]):
        out_ref[k] = (own_ref[k] + other_ref[k].astype(F32)).astype(BF16)


def line_sum_kernel(parts_ref, out_ref):
    total = parts_ref[0].astype(F32)
    for k in range(1, parts_ref.shape[0]):
        total = total + parts_ref[k].astype(F32)
    out_ref[...] = total


def copies_kernel(halves_ref, out_ref):
    total = (halves_ref[0].astype(F32) + halves_ref[1].astype(F32)).astype(BF16)
    for k in range(out_ref.shape[0]):
        out_ref[k] = total


def shape(dims, dtype=F32):
    return jax.ShapeDtypeStruct(dims, dtype)


def to_all(block, axis):
    count = lax.axis_size(axis)
    return lax.all_to_all(jnp.broadcast_to(block[None], (count,) + block.shape), axis, 0, 0)


def flip(block, axis, bit):
    return lax.ppermute(block, axis, [(k, k ^ bit) for k in range(lax.axis_size(axis))])


def swap(block, axis):
    return flip(block, axis, 1)


def on_device(layer_input, proj_weight, ssd_input, log_decay, out_grad):
    steps, width = layer_input.shape
    heads = log_decay.shape[1]
    slabs = lax.axis_size(TM)
    groups = lax.axis_size("z")
    rows_here = proj_weight.shape[0]
    core = lax.axis_index("core").reshape(1)
    share = ssd_input.shape[1] // slabs
    logt = log_decay.T

    line_w = to_all(proj_weight, "ylo")
    own_w = to_all(line_w, "x").reshape(-1, rows_here, width)
    other_w = swap(own_w, "core")
    xet, dyft, ds = call(
        prepare,
        (
            shape(ssd_input.shape[::-1]),
            shape(ssd_input.shape[::-1]),
            shape((heads, N)),
        ),
        10**7,
        ssd_input,
        out_grad,
        log_decay,
        logt,
    )
    other_w, xet, dyft, ds = lax.optimization_barrier((other_w, xet, dyft, ds))
    partial = call(
        partial_kernel,
        shape((groups, steps + EXTRA_ROWS, 2 * N)),
        2 * steps * width * slabs * rows_here,
        core,
        layer_input,
        own_w,
        other_w,
        smem=1,
    )
    pieces = lax.all_to_all(partial.astype(F16), "z", 0, 0).astype(F32)
    half_bc = call(sum_kernel, shape((steps + EXTRA_ROWS, 2 * N)), 10**6, pieces).astype(F16)
    halves = lax.all_gather(half_bc, "yhi").astype(F32)

    parts = call(
        states_kernel,
        shape((slabs, 2 * share + EXTRA_ROWS, N)),
        12 * steps * N * ssd_input.shape[1],
        halves,
        xet,
        dyft,
        ds,
    )
    shares = lax.all_to_all(parts.astype(F16), TM, 0, 0).astype(F32)
    gx, terms, inside = call(
        local_kernel,
        (
            shape(ssd_input.shape),
            shape((steps, 2 * (ssd_input.shape[1] + N)), BF16),
            shape((heads, steps)),
        ),
        10**8,
        halves,
        ssd_input,
        out_grad,
        log_decay,
        logt,
    )
    carried = call(scan_kernel, shape(shares.shape, BF16), 10**6, shares)
    arrived = lax.all_to_all(carried, TM, 0, 0)
    own_grad = call(
        bc_grad_kernel,
        shape((2 * N, steps), BF16),
        4 * steps * N * ssd_input.shape[1],
        arrived,
        terms,
    )
    near_input, _ = lax.optimization_barrier((layer_input, carried))
    pair = jnp.concatenate([near_input, flip(near_input, "x", 1)], axis=0)
    own_grad, pair = lax.optimization_barrier((own_grad, pair))
    halves_grad = lax.all_gather(own_grad, "yhi")
    grad_x, grad_log = call(
        finish_kernel,
        (shape(ssd_input.shape), shape((heads, steps))),
        10**8,
        arrived,
        halves,
        ssd_input,
        out_grad,
        log_decay,
        logt,
        gx,
        inside,
    )
    copies = call(copies_kernel, shape((groups, 2 * N, steps), BF16), 10**6, halves_grad)
    all_grads = lax.all_to_all(copies, "z", 0, 0)
    pair, _ = lax.optimization_barrier((pair, copies))
    far_pair = flip(pair, "x", 2)
    all_grads, pair, far_pair, grad_x, grad_log = lax.optimization_barrier(
        (all_grads, pair, far_pair, grad_x, grad_log)
    )
    columns = groups // 2
    blocks = call(
        row_blocks_kernel, shape((4, 2 * columns, rows_here, steps), BF16), 10**6, all_grads
    )
    row_grads = lax.all_to_all(blocks, "x", 0, 0)
    keep, send = call(
        grad_weight_kernel,
        (shape((columns, rows_here, width)), shape((columns, rows_here, width), BF16)),
        2 * steps * width * slabs * rows_here,
        jnp.concatenate([core, lax.axis_index("x").reshape(1)]),
        row_grads,
        pair,
        far_pair,
        smem=1,
    )
    from_core = swap(send, "core")
    all_grads, _ = lax.optimization_barrier((all_grads, send))
    grad_input = call(
        grad_input_kernel,
        shape(layer_input.shape, BF16),
        2 * steps * width * slabs * rows_here,
        core,
        all_grads,
        own_w,
        other_w,
        smem=1,
    )
    from_core, grad_input = lax.optimization_barrier((from_core, grad_input))
    of_chip = call(chip_sum_kernel, shape(send.shape, BF16), 10**6, keep, from_core)
    of_line = lax.all_to_all(of_chip, "ylo", 0, 0)
    grad_weight = call(line_sum_kernel, shape(proj_weight.shape), 10**6, of_line)
    return grad_x, grad_log.T, grad_input, grad_weight


def solution(mesh):
    fine = Mesh(mesh.devices.reshape(4, 4, 2, 8, 2), TM + HEADS)
    spec = P(TM, HEADS)
    return jax.shard_map(
        on_device,
        mesh=fine,
        in_specs=(spec,) * 5,
        out_specs=(spec,) * 4,
        check_vma=False,
    )
```

```python
import jax
import jax.numpy as jnp
from jax import lax
from jax.experimental import pallas as pl
from jax.experimental.pallas import tpu as pltpu
from jax.sharding import Mesh
from jax.sharding import PartitionSpec as P

N = 128
EXTRA_ROWS = 8
LN2 = 0.6931471805599453
SCALE = 256.0
F32 = jnp.float32
BF16 = jnp.bfloat16
F16 = jnp.float16
HIGHEST = lax.Precision.HIGHEST
TM = ("ylo", "x", "core")
HEADS = ("z", "yhi")


def dot(a, b, precision=None):
    return jnp.dot(a, b, preferred_element_type=F32, precision=precision)


def dot_nt(a, b, precision=None):
    return lax.dot_general(
        a, b, (((1,), (1,)), ((), ())), preferred_element_type=F32, precision=precision
    )


def dot_tn(a, b):
    return lax.dot_general(a, b, (((0,), (0,)), ((), ())), preferred_element_type=F32)


def split(a):
    high = a.astype(BF16)
    return high, (a - high.astype(F32)).astype(BF16)


def dot_split(a, b):
    a_high, a_low = split(a)
    b_high, b_low = split(b)
    return dot(a_high, b_high) + dot(a_low, b_high) + dot(a_high, b_low)


def three_terms(row):
    high = row.astype(BF16).astype(F32)
    middle = (row - high).astype(BF16).astype(F32)
    low = row - high - middle
    term = lax.broadcasted_iota(jnp.int32, (EXTRA_ROWS, N), 0)
    return jnp.where(
        term == 0, high, jnp.where(term == 1, middle, jnp.where(term == 2, low, 0.0))
    )


def exponent_of(a):
    top = jnp.max(jnp.max(jnp.abs(a), axis=1, keepdims=True), axis=0, keepdims=True)
    return jnp.ceil(jnp.log(jnp.maximum(top, 1e-30)) * (1.0 / LN2)) - 14.0


def power(exponent):
    return jnp.exp(exponent * LN2)


def iotas(n):
    return (
        lax.broadcasted_iota(jnp.int32, (n, n), 0),
        lax.broadcasted_iota(jnp.int32, (n, n), 1),
    )


def head_spread(heads, width):
    size = width // heads
    row = lax.broadcasted_iota(jnp.int32, (heads, width), 0)
    col = lax.broadcasted_iota(jnp.int32, (heads, width), 1)
    return ((col >= row * size) & (col < (row + 1) * size)).astype(F32)


def call(kernel, outs, flops, *args, smem=0):
    out_list = outs if isinstance(outs, tuple) else (outs,)
    read = sum(a.size * a.dtype.itemsize for a in args)
    wrote = sum(o.size * o.dtype.itemsize for o in out_list)
    spaces = [pltpu.SMEM if k < smem else pltpu.VMEM for k in range(len(args))]
    return pl.pallas_call(
        kernel,
        out_shape=outs,
        in_specs=[pl.BlockSpec(memory_space=space) for space in spaces],
        out_specs=jax.tree.map(lambda _: pl.BlockSpec(memory_space=pltpu.VMEM), outs),
        cost_estimate=pl.CostEstimate(
            flops=flops, bytes_accessed=read + wrote, transcendentals=0
        ),
        compiler_params=pltpu.CompilerParams(vmem_limit_bytes=16 * 2**20),
    )(*args)


def decay_sums(log_ref, logt_ref):
    row, col = iotas(log_ref.shape[0])
    cum = dot((row >= col).astype(F32), log_ref[...], HIGHEST)
    cumt = dot(logt_ref[...], (row <= col).astype(F32), HIGHEST)
    return cum, cumt


def decay_factors(cum, width):
    spread = head_spread(cum.shape[1], width)
    last = cum[cum.shape[0] - 1 :, :]
    return dot(jnp.exp(last - cum), spread, HIGHEST), dot(jnp.exp(cum), spread, HIGHEST)


def prepare(x_ref, dy_ref, log_ref, logt_ref, xet_ref, dyft_ref, ds_ref):
    steps = log_ref.shape[0]
    cum, cumt = decay_sums(log_ref, logt_ref)
    to_end, from_start = decay_factors(cum, x_ref.shape[1])
    xet_ref[...] = (x_ref[...] * to_end).T
    dyft_ref[...] = (dy_ref[...] * from_start).T
    ds_ref[...] = jnp.broadcast_to(cumt[:, steps - 1 : steps], ds_ref.shape)


def blocks_of(first, own_ref, other_ref, group, lines):
    column, half = divmod(group, 2)
    rows = []
    for line in (2 * half, 2 * half + 1):
        at = line * lines + column
        own, other = own_ref[at], other_ref[at]
        rows += [jnp.where(first, own, other), jnp.where(first, other, own)]
    return jnp.concatenate(rows, axis=0)


def partial_kernel(core_ref, x_ref, own_ref, other_ref, out_ref):
    first = core_ref[0] == 0
    x = x_ref[...]
    steps = x.shape[0]
    groups, _, columns = out_ref.shape
    for group in range(groups):
        part = dot_nt(x, blocks_of(first, own_ref, other_ref, group, groups // 2))
        exponent = exponent_of(part)
        out_ref[group, :steps, :] = part * power(-exponent)
        out_ref[group, steps:, :] = jnp.broadcast_to(exponent, (EXTRA_ROWS, columns))


def sum_kernel(pieces_ref, out_ref):
    pieces, rows, columns = pieces_ref.shape
    steps = rows - EXTRA_ROWS
    exponents = [pieces_ref[k, steps:, :] for k in range(pieces)]
    top = exponents[0]
    for exponent in exponents[1:]:
        top = jnp.maximum(top, exponent)
    top = top + jnp.ceil(jnp.log(1.0 * pieces) / LN2)
    total = jnp.zeros((steps, columns), F32)
    for k in range(pieces):
        total = total + pieces_ref[k, :steps, :] * power(exponents[k] - top)[:1, :]
    out_ref[:steps, :] = total
    out_ref[steps:, :] = top


def whole_bc(halves_ref):
    steps = halves_ref.shape[1] - EXTRA_ROWS
    bc = sum(
        halves_ref[k, :steps, :] * power(halves_ref[k, steps : steps + 1, :]) for k in range(2)
    )
    return bc[:, :N], bc[:, N:]


def states_kernel(halves_ref, xet_ref, dyft_ref, ds_ref, out_ref):
    b_rows, c_rows = whole_bc(halves_ref)
    heads = ds_ref.shape[0]
    parts, rows, _ = out_ref.shape
    half = (rows - EXTRA_ROWS) // 2
    state = dot_split(xet_ref[...], b_rows)
    grad = dot_split(dyft_ref[...], c_rows)
    state_exponent = exponent_of(state)
    grad_exponent = exponent_of(grad)
    out_ref[:, :half, :] = (state * power(-state_exponent)).reshape(parts, half, N)
    out_ref[:, half : 2 * half, :] = (grad * power(-grad_exponent)).reshape(parts, half, N)
    row = lax.broadcasted_iota(jnp.int32, (EXTRA_ROWS, N), 0)
    for head in range(heads):
        terms = jnp.where(row == 3, state_exponent, three_terms(SCALE * ds_ref[head : head + 1, :]))
        terms = jnp.where(row == 4, grad_exponent, terms)
        for part in range(head * parts // heads, (head + 1) * parts // heads):
            out_ref[part, 2 * half :, :] = terms


def local_kernel(halves_ref, x_ref, dy_ref, log_ref, logt_ref, gx_ref, terms_ref, inside_ref):
    b_rows, c_rows = (rows.astype(BF16) for rows in whole_bc(halves_ref))
    steps, heads = log_ref.shape
    size = x_ref.shape[1] // heads
    row, col = iotas(steps)
    later = row <= col
    at_or_after = (row >= col).astype(BF16)
    bct = dot_nt(b_rows, c_rows)
    pair_sum = jnp.zeros((steps, steps), F32)
    cum, cumt = decay_sums(log_ref, logt_ref)
    for h in range(heads):
        x = x_ref[:, h * size : (h + 1) * size].astype(BF16)
        dy = dy_ref[:, h * size : (h + 1) * size].astype(BF16)
        gap = cumt[h : h + 1, :] - cum[:, h : h + 1]
        decay = jnp.where(later, jnp.exp(jnp.minimum(gap, 0.0)), 0.0)
        decayed = decay * dot_nt(x, dy)
        pair_sum = pair_sum + decayed
        gx_ref[:, h * size : (h + 1) * size] = dot((decay * bct).astype(BF16), dy)
        reach = dot((decayed * bct).astype(BF16), at_or_after)
        inside_ref[h : h + 1, :] = jnp.sum(jnp.where(row < col, reach, 0.0), axis=0, keepdims=True)
    width = x_ref.shape[1]
    to_end, from_start = decay_factors(cum, width)
    terms_ref[:, :width] = (x_ref[...] * to_end).astype(BF16)
    terms_ref[:, width : 2 * width] = (dy_ref[...] * from_start).astype(BF16)
    terms_ref[:, 2 * width : 2 * width + N] = dot(pair_sum.astype(BF16), c_rows).astype(BF16)
    terms_ref[:, 2 * width + N :] = dot(pair_sum.T.astype(BF16), b_rows).astype(BF16)


def scan_kernel(parts_ref, out_ref):
    slabs, rows, _ = out_ref.shape
    rows -= EXTRA_ROWS
    half = rows // 2

    def extra(t, k):
        return parts_ref[t, rows + k : rows + k + 1, :]

    decays = [jnp.exp((extra(t, 0) + extra(t, 1) + extra(t, 2)) / SCALE) for t in range(slabs)]
    grads = [jnp.zeros((half, N), F32)]
    for t in range(slabs - 1, 0, -1):
        grads.append(decays[t] * grads[-1] + power(extra(t, 4)) * parts_ref[t, half:rows, :])
    grads = grads[::-1]
    state = jnp.zeros((half, N), F32)
    for t in range(slabs):
        out_ref[t, :half, :] = state.astype(BF16)
        out_ref[t, half:rows, :] = grads[t].astype(BF16)
        product = jnp.sum(state * grads[t], axis=0, keepdims=True)
        out_ref[t, rows:, :] = three_terms(product).astype(BF16)
        state = decays[t] * state + power(extra(t, 3)) * parts_ref[t, :half, :]


def entering(in_ref):
    parts, rows, _ = in_ref.shape
    half = (rows - EXTRA_ROWS) // 2
    state = in_ref[:, :half, :].reshape(parts * half, N)
    grad = in_ref[:, half : 2 * half, :].reshape(parts * half, N)
    return state, grad


def bc_grad_kernel(in_ref, terms_ref, out_ref):
    state, grad = entering(in_ref)
    width = state.shape[0]
    from_grad = dot(terms_ref[:, :width], grad)
    from_state = dot(terms_ref[:, width : 2 * width], state)
    out_ref[:N, :] = (terms_ref[:, 2 * width : 2 * width + N].astype(F32) + from_grad).T.astype(BF16)
    out_ref[N:, :] = (terms_ref[:, 2 * width + N :].astype(F32) + from_state).T.astype(BF16)


def finish_kernel(in_ref, halves_ref, x_ref, dy_ref, log_ref, logt_ref, gx_ref, inside_ref, out_ref, out_log_ref):
    state, grad = entering(in_ref)
    b_rows, c_rows = (rows.astype(BF16) for rows in whole_bc(halves_ref))
    steps, heads = log_ref.shape
    width = x_ref.shape[1]
    row, col = iotas(steps)
    cum, cumt = decay_sums(log_ref, logt_ref)
    to_end, from_start = decay_factors(cum, width)
    b_state = to_end * dot_nt(b_rows, grad)
    c_state = from_start * dot_nt(c_rows, state)
    out_ref[...] = gx_ref[...] + b_state
    spread = head_spread(heads, width)
    earlier = dot_nt(spread, c_state * dy_ref[...], HIGHEST)
    later = dot_nt(spread, b_state * x_ref[...], HIGHEST)
    parts = in_ref.shape[0]
    products = jnp.sum(in_ref[:, -EXTRA_ROWS:, :].astype(F32), axis=1)
    products = jnp.sum(products.reshape(heads, parts // heads, N), axis=1)
    across = jnp.sum(products, axis=1, keepdims=True)
    across = across * jnp.exp(cumt[:, steps - 1 : steps])
    out_log_ref[...] = (
        inside_ref[...]
        + dot(earlier, (row >= col).astype(F32), HIGHEST)
        + dot(later, (row < col).astype(F32), HIGHEST)
        + across
    )


def grad_input_kernel(core_ref, grads_ref, own_ref, other_ref, out_ref):
    first = core_ref[0] == 0
    groups = grads_ref.shape[0]
    total = jnp.zeros(out_ref.shape, F32)
    for group in range(groups):
        rows = blocks_of(first, own_ref, other_ref, group, groups // 2)
        total = total + dot_tn(grads_ref[group], rows)
    out_ref[...] = total.astype(BF16)


def row_blocks_kernel(grads_ref, out_ref):
    lines, _, rows, _ = out_ref.shape
    for group in range(grads_ref.shape[0]):
        column, high = divmod(group, 2)
        for k in range(2):
            for core in range(2):
                at = (2 * k + core) * rows
                out_ref[2 * high + k, 2 * column + core] = grads_ref[group, at : at + rows, :]


def half_weight(place_ref, grads_ref, x_ref, column, blocks, rows):
    grads = [
        grads_ref[place_ref[1] ^ k, 2 * column : 2 * column + 2].reshape(2 * rows, -1)
        for k in blocks
    ]
    return dot(jnp.concatenate(grads, axis=1), x_ref[...])


def near_weight_kernel(place_ref, grads_ref, x_ref, out_ref):
    for column in range(out_ref.shape[0]):
        out_ref[column] = half_weight(place_ref, grads_ref, x_ref, column, (0, 1), grads_ref.shape[2])


def grad_weight_kernel(place_ref, grads_ref, x_ref, near_ref, keep_ref, send_ref):
    first = place_ref[0] == 0
    columns, rows, _ = keep_ref.shape
    for column in range(columns):
        part = near_ref[column] + half_weight(place_ref, grads_ref, x_ref, column, (2, 3), rows)
        one, other = part[:rows], part[rows:]
        keep_ref[column] = jnp.where(first, one, other)
        send_ref[column] = jnp.where(first, other, one).astype(BF16)


def chip_sum_kernel(own_ref, other_ref, out_ref):
    for k in range(out_ref.shape[0]):
        out_ref[k] = (own_ref[k] + other_ref[k].astype(F32)).astype(BF16)


def line_sum_kernel(parts_ref, out_ref):
    total = parts_ref[0].astype(F32)
    for k in range(1, parts_ref.shape[0]):
        total = total + parts_ref[k].astype(F32)
    out_ref[...] = total


def copies_kernel(halves_ref, out_ref):
    total = (halves_ref[0].astype(F32) + halves_ref[1].astype(F32)).astype(BF16)
    for k in range(out_ref.shape[0]):
        out_ref[k] = total


def shape(dims, dtype=F32):
    return jax.ShapeDtypeStruct(dims, dtype)


def to_all(block, axis):
    count = lax.axis_size(axis)
    return lax.all_to_all(jnp.broadcast_to(block[None], (count,) + block.shape), axis, 0, 0)


def flip(block, axis, bit):
    return lax.ppermute(block, axis, [(k, k ^ bit) for k in range(lax.axis_size(axis))])


def swap(block, axis):
    return flip(block, axis, 1)


def on_device(layer_input, proj_weight, ssd_input, log_decay, out_grad):
    steps, width = layer_input.shape
    heads = log_decay.shape[1]
    slabs = lax.axis_size(TM)
    groups = lax.axis_size("z")
    rows_here = proj_weight.shape[0]
    core = lax.axis_index("core").reshape(1)
    share = ssd_input.shape[1] // slabs
    logt = log_decay.T

    line_w = to_all(proj_weight, "ylo")
    own_w = to_all(line_w, "x").reshape(-1, rows_here, width)
    other_w = swap(own_w, "core")
    xet, dyft, ds = call(
        prepare,
        (
            shape(ssd_input.shape[::-1]),
            shape(ssd_input.shape[::-1]),
            shape((heads, N)),
        ),
        10**7,
        ssd_input,
        out_grad,
        log_decay,
        logt,
    )
    other_w, xet, dyft, ds = lax.optimization_barrier((other_w, xet, dyft, ds))
    partial = call(
        partial_kernel,
        shape((groups, steps + EXTRA_ROWS, 2 * N)),
        2 * steps * width * slabs * rows_here,
        core,
        layer_input,
        own_w,
        other_w,
        smem=1,
    )
    pieces = lax.all_to_all(partial.astype(F16), "z", 0, 0).astype(F32)
    half_bc = call(sum_kernel, shape((steps + EXTRA_ROWS, 2 * N)), 10**6, pieces).astype(F16)
    halves = lax.all_gather(half_bc, "yhi").astype(F32)

    parts = call(
        states_kernel,
        shape((slabs, 2 * share + EXTRA_ROWS, N)),
        12 * steps * N * ssd_input.shape[1],
        halves,
        xet,
        dyft,
        ds,
    )
    shares = lax.all_to_all(parts.astype(F16), TM, 0, 0).astype(F32)
    gx, terms, inside = call(
        local_kernel,
        (
            shape(ssd_input.shape),
            shape((steps, 2 * (ssd_input.shape[1] + N)), BF16),
            shape((heads, steps)),
        ),
        10**8,
        halves,
        ssd_input,
        out_grad,
        log_decay,
        logt,
    )
    carried = call(scan_kernel, shape(shares.shape, BF16), 10**6, shares)
    arrived = lax.all_to_all(carried, TM, 0, 0)
    own_grad = call(
        bc_grad_kernel,
        shape((2 * N, steps), BF16),
        4 * steps * N * ssd_input.shape[1],
        arrived,
        terms,
    )
    near_input, _ = lax.optimization_barrier((layer_input, carried))
    pair = jnp.concatenate([near_input, flip(near_input, "x", 1)], axis=0)
    own_grad, pair = lax.optimization_barrier((own_grad, pair))
    halves_grad = lax.all_gather(own_grad, "yhi")
    grad_x, grad_log = call(
        finish_kernel,
        (shape(ssd_input.shape), shape((heads, steps))),
        10**8,
        arrived,
        halves,
        ssd_input,
        out_grad,
        log_decay,
        logt,
        gx,
        inside,
    )
    copies = call(copies_kernel, shape((groups, 2 * N, steps), BF16), 10**6, halves_grad)
    all_grads = lax.all_to_all(copies, "z", 0, 0)
    pair, _ = lax.optimization_barrier((pair, copies))
    far_pair = flip(pair, "x", 2)
    all_grads, pair, far_pair, grad_x, grad_log = lax.optimization_barrier(
        (all_grads, pair, far_pair, grad_x, grad_log)
    )
    columns = groups // 2
    blocks = call(
        row_blocks_kernel, shape((4, 2 * columns, rows_here, steps), BF16), 10**6, all_grads
    )
    row_grads = lax.all_to_all(blocks, "x", 0, 0)
    place = jnp.concatenate([core, lax.axis_index("x").reshape(1)])
    near_weight = call(
        near_weight_kernel,
        shape((columns, 2 * rows_here, width)),
        steps * width * slabs * rows_here,
        place,
        row_grads,
        pair,
        smem=1,
    )
    keep, send = call(
        grad_weight_kernel,
        (shape((columns, rows_here, width)), shape((columns, rows_here, width), BF16)),
        steps * width * slabs * rows_here,
        place,
        row_grads,
        far_pair,
        near_weight,
        smem=1,
    )
    from_core = swap(send, "core")
    all_grads, _ = lax.optimization_barrier((all_grads, send))
    grad_input = call(
        grad_input_kernel,
        shape(layer_input.shape, BF16),
        2 * steps * width * slabs * rows_here,
        core,
        all_grads,
        own_w,
        other_w,
        smem=1,
    )
    from_core, grad_input = lax.optimization_barrier((from_core, grad_input))
    of_chip = call(chip_sum_kernel, shape(send.shape, BF16), 10**6, keep, from_core)
    of_line = lax.all_to_all(of_chip, "ylo", 0, 0)
    grad_weight = call(line_sum_kernel, shape(proj_weight.shape), 10**6, of_line)
    return grad_x, grad_log.T, grad_input, grad_weight


def solution(mesh):
    fine = Mesh(mesh.devices.reshape(4, 4, 2, 8, 2), TM + HEADS)
    spec = P(TM, HEADS)
    return jax.shard_map(
        on_device,
        mesh=fine,
        in_specs=(spec,) * 5,
        out_specs=(spec,) * 4,
        check_vma=False,
    )
```
